512 devices in a mesh: blk: 64 (over z_lo, y, core), txt: 8 (over z_hi, x).
Axes of the slice: x: 4, y: 8, z: 8 (z_hi: 2, z_lo: 4; z = z_hi * 4 + z_lo), core: 2. Of those that a mesh axis runs over, the one named last changes fastest.
Arguments:
- image_student: bfloat16 [8192, 768], P('blk'), may hold values from -40 to 40
- head_weight: bfloat16 [768, 768], replicated, may hold values from -0.21875 to 0.21875
- text_student: bfloat16 [8192, 768], P(('blk', 'txt')), may hold values from -0.8 to 0.8
- image_teacher: bfloat16 [8192, 1152], P('blk'), may hold values from -40 to 40
- text_teacher: bfloat16 [8192, 1152], P(('blk', 'txt')), may hold values from -40 to 40
- logit_scales: float32 [2], replicated, may hold values from 5 to 15
- logit_biases: float32 [2], replicated, may hold values from -4 to -1
- loss_scale: float32 [1], replicated, may hold values from 256 to 1024
Outputs:
- head_grad: float32 [768, 768], P('blk')
- text_grad: float32 [8192, 768], P(('blk', 'txt'))
- row_loss: float32 [8192], P('blk')
The draws below stay inside these ranges and needn't reach their ends.
All inputs are finite; a program needn't handle non-finite values.
Results may differ from the reference program's by a relative error of at most 0.0039.
Values may be sent and summed in bfloat16 or wider, within the bound.
A program may use at most 64 MiB of HBM per device.

```python
import math
import jax
import jax.numpy as jnp
from jax import lax

D = 768
DT = 1152
IMG_ROWS = 128
BATCH = 8192
N_BLK = 64


def spread_scale(key, values, base):
    key = jax.random.fold_in(key, 5)
    keys = jax.random.split(key, 2)
    row_scale = jnp.exp(jax.random.uniform(keys[0], (values.shape[0], 1), minval=0.0, maxval=0.5 * math.log(10.0)))
    col_scale = jnp.exp(jax.random.uniform(keys[1], (1, values.shape[1]), minval=0.0, maxval=0.5 * math.log(10.0)))
    return base * jnp.clip(values, -4.0, 4.0) * row_scale * col_scale


def draw_image_student(key, part):
    key = jax.random.fold_in(key, 11)
    values = jax.random.normal(key, (BATCH, D))
    return spread_scale(key, values, 1.0).astype(jnp.bfloat16)


def draw_text_student(key, part):
    key = jax.random.fold_in(key, 12)
    values = jax.random.normal(key, (BATCH, D))
    return spread_scale(key, values, 0.02).astype(jnp.bfloat16)


def draw_image_teacher(key, part):
    key = jax.random.fold_in(key, 13)
    values = jax.random.normal(key, (BATCH, DT))
    return spread_scale(key, values, 1.0).astype(jnp.bfloat16)


def draw_text_teacher(key, part):
    key = jax.random.fold_in(key, 14)
    values = jax.random.normal(key, (BATCH, DT))
    return spread_scale(key, values, 1.0).astype(jnp.bfloat16)


def noise(stream_key, dims, scale, limit, kind=jnp.bfloat16):
    return jnp.clip(scale * jax.random.normal(stream_key, dims, jnp.float32), -limit, limit).astype(kind)


def setup_inputs(seed: int = 0) -> dict:
    arg_keys = jax.random.split(jax.random.key(seed), 9)
    image_student = draw_image_student(jax.random.fold_in(arg_keys[8], 71), 0)
    head_weight = noise(arg_keys[1], (D, D), D ** -0.5, 0.21875)
    text_student = draw_text_student(jax.random.fold_in(arg_keys[8], 71), 0)
    image_teacher = draw_image_teacher(jax.random.fold_in(arg_keys[8], 71), 0)
    text_teacher = draw_text_teacher(jax.random.fold_in(arg_keys[8], 71), 0)
    logit_scales = jnp.clip(jnp.exp(jax.random.uniform(arg_keys[5], (2,), jnp.float32, math.log(5.0), math.log(15.0))), 5.0, 15.0)
    logit_biases = jnp.clip(jax.random.uniform(arg_keys[6], (2,), jnp.float32, -4.0, -1.0), -4.0, -1.0)
    loss_scale = jnp.clip(jnp.exp(jax.random.uniform(arg_keys[7], (1,), jnp.float32, math.log(256.0), math.log(1024.0))), 256.0, 1024.0)
    return dict(image_student=image_student, head_weight=head_weight, text_student=text_student, image_teacher=image_teacher, text_teacher=text_teacher, logit_scales=logit_scales, logit_biases=logit_biases, loss_scale=loss_scale)


epsilon = 1e-06

def normalize(matrix):
    widened = matrix.astype(jnp.float32)
    radius = jnp.sqrt(lax.optimization_barrier(jnp.sum(widened * widened, axis=1, keepdims=True)) + epsilon)
    return (widened / radius, radius)

def pull_back(grad_unit, unit_rows, radius):
    radial = lax.optimization_barrier(jnp.sum(grad_unit * unit_rows, axis=1, keepdims=True))
    return (grad_unit - unit_rows * radial) / radius

def reference(image_student, head_weight, text_student, image_teacher, text_teacher, logit_scales, logit_biases, loss_scale):
    projected = jnp.dot(image_student, head_weight, preferred_element_type=jnp.float32)
    image_unit, image_radius = normalize(projected)
    image_low = image_unit.astype(jnp.bfloat16)
    text_unit, text_radius = normalize(text_student)
    text_low = text_unit.astype(jnp.bfloat16)
    teach_image = normalize(image_teacher)[0].astype(jnp.bfloat16)
    teach_text = normalize(text_teacher)[0].astype(jnp.bfloat16)
    factor = loss_scale[0] * logit_scales[0] / BATCH
    image_blocks = image_low.reshape(N_BLK, IMG_ROWS, D)
    teach_blocks = teach_image.reshape(N_BLK, IMG_ROWS, DT)

    def visit(text_acc, pieces):
        image_block, teach_block = pieces
        student = logit_scales[0] * jnp.dot(image_block, text_low.T, preferred_element_type=jnp.float32) + logit_biases[0]
        teacher = logit_scales[1] * jnp.dot(teach_block, teach_text.T, preferred_element_type=jnp.float32) + logit_biases[1]
        target = jax.nn.sigmoid(teacher)
        pair_loss = jax.nn.softplus(student) - target * student
        row_part = lax.optimization_barrier(jnp.sum(pair_loss, axis=1)) / BATCH
        errors = (jax.nn.sigmoid(student) - target).astype(jnp.bfloat16)
        image_part = factor * jnp.dot(errors, text_low, preferred_element_type=jnp.float32)
        text_acc = text_acc + factor * jnp.dot(errors.T, image_block, preferred_element_type=jnp.float32)
        return (text_acc, (row_part, image_part))
    text_acc, outputs = lax.scan(visit, jnp.zeros((BATCH, D), jnp.float32), (image_blocks, teach_blocks))
    row_loss = outputs[0].reshape(BATCH)
    image_grad = outputs[1].reshape(BATCH, D)
    image_step = pull_back(image_grad, image_unit, image_radius)
    head_grad = jnp.dot(image_student.astype(jnp.float32).T, image_step, precision=lax.Precision.HIGHEST)
    text_grad = pull_back(text_acc, text_unit, text_radius)
    return (head_grad, text_grad, row_loss)
```

```python
import jax
import jax.numpy as jnp
from jax import lax
from jax.experimental import pallas as pl
from jax.experimental.pallas import tpu as pltpu
from jax.sharding import PartitionSpec as P

epsilon = 1e-06
MESH = pl.DeviceIdType.MESH
f32 = jnp.float32
bf16 = jnp.bfloat16

FLOW = {1: (1, 1), 2: (1, -1), 3: (2, 1), 4: (2, -1), 5: (3, 1), 6: (3, -1), 7: (4, 1)}
NEXT = {1: 3, 2: 4, 3: 5, 4: 6, 5: 7}
GROUPS = [(0, 1), (1, 2), (3, 2), (5, 2), (7, 1)]
ZFLOW = {1: 1, 2: -1, 3: 2}


def contract_last(a, b):
    return lax.dot_general(a, b, (((1,), (1,)), ((), ())), preferred_element_type=f32)


def contract_first(a, b):
    return lax.dot_general(a, b, (((0,), (0,)), ((), ())), preferred_element_type=f32)


class Tags:
    def __init__(self):
        self.index = {}

    def __call__(self, *key):
        return self.index.setdefault(key, len(self.index))


MESSAGES = 128


def kernel(
    x_hbm, w_hbm, ts_hbm, xt_hbm, tt_hbm, scales, biases, loss_scale,
    head_out, text_out, loss_out,
    xall, xtall, w, ts, tt, sb, tb, unit, low, rad, teach, xtp,
    err, town, zs, zr, ysend, yr, grad, sfull, crecv, csum, sx, xr, hsum, hb, hr, zb, zrec, ag, lpart, lc, lx, lxr, lh,
    local_sem, send_sem, recv_sem,
):
    blk = lax.axis_index("blk")
    txt = lax.axis_index("txt")
    x = lax.rem(txt, 4)
    c = lax.rem(blk, 2)
    y = lax.rem(blk // 2, 8)
    z = (txt // 4) * 4 + blk // 16
    sgn = 2 * c - 1

    def at(dx=0, dy=0, dz=0, core=c):
        xx = lax.rem(x + dx + 8, 4)
        yy = lax.rem(y + dy + 16, 8)
        zz = lax.rem(z + dz + 16, 8)
        return {"blk": (lax.rem(zz, 4) * 8 + yy) * 2 + core, "txt": (zz // 4) * 4 + xx}

    loads = [
        pltpu.make_async_copy(ts_hbm, ts, local_sem.at[0]),
        pltpu.make_async_copy(tt_hbm, tt, local_sem.at[1]),
        pltpu.make_async_copy(x_hbm, xall.at[c], local_sem.at[2]),
        pltpu.make_async_copy(xt_hbm, xtall.at[c], local_sem.at[3]),
        pltpu.make_async_copy(w_hbm, w, local_sem.at[4]),
    ]
    for copy in loads:
        copy.start()

    barrier = pltpu.get_barrier_semaphore()
    partners = [at(core=1 - c)]
    partners += [at(dx=r, core=k) for r in (1, 2, 3) for k in (c, 1 - c)]
    partners += [at(dy=r) for r in range(1, 8)]
    partners += [at(dz=r) for r in range(1, 8)]
    for partner in partners:
        pl.semaphore_signal(barrier, inc=1, device_id=partner, device_id_type=MESH)

    tags = Tags()

    def message(key, src, dst, device):
        index = tags(*key)
        assert index < MESSAGES
        return pltpu.make_async_remote_copy(
            src, dst, send_sem.at[index], recv_sem.at[index], device_id=device, device_id_type=MESH
        )

    sent = []

    def send(key, src, dst, device):
        copy = message(key, src, dst, device)
        copy.start()
        sent.append(copy)

    def arrive(key, dst):
        message(key, dst, dst, at()).wait_recv()

    loads[0].wait()
    loads[1].wait()
    t_wide = ts[...].astype(f32)
    t_rad = jnp.sqrt(jnp.sum(t_wide * t_wide, axis=1, keepdims=True) + epsilon)
    t_unit = t_wide / t_rad
    sb[0, 0] = t_unit.astype(bf16)
    q_wide = tt[...].astype(f32)
    tb[0, 0] = (q_wide / jnp.sqrt(jnp.sum(q_wide * q_wide, axis=1, keepdims=True) + epsilon)).astype(bf16)

    pl.semaphore_wait(barrier, len(partners))

    y_to = {1: at(dy=sgn), -1: at(dy=-sgn)}
    z_to = {1: at(dz=sgn), -1: at(dz=-sgn)}
    sibling = at(core=1 - c)

    def s_part(pos, part):
        return sb.at[pos, pl.ds(0, 1)] if part == 0 else sb.at[pos, pl.ds(1, 2)] if part == 1 else sb.at[pos, pl.ds(3, 1)]

    def t_group(b, group):
        start, count = GROUPS[group]
        return tb.at[b, pl.ds(start, count)]

    def send_s_y(pos_from, part):
        targets = [(1, 1), (2, -1)] if pos_from == 0 else [(NEXT[pos_from], FLOW[pos_from][1])] if pos_from in NEXT else []
        for pos, sign in targets:
            send(("sy", pos, part), s_part(pos_from, part), s_part(pos, part), y_to[sign])

    def send_t_y(pos_from):
        targets = [(1, 1), (2, -1)] if pos_from == 0 else [(NEXT[pos_from], FLOW[pos_from][1])] if pos_from in NEXT else []
        for pos, sign in targets:
            send(("ty", pos), tb.at[0, pos_from], tb.at[0, pos], y_to[sign])

    def send_t_z(group):
        send(("tz", 1, group), t_group(0, group), t_group(1, group), z_to[1])
        send(("tz", 2, group), t_group(0, group), t_group(2, group), z_to[-1])

    send_t_y(0)
    send(("sz", 1), sb.at[0, 0], sb.at[0, 1], z_to[1])
    send(("sz", 2), sb.at[0, 0], sb.at[0, 2], z_to[-1])
    send_s_y(0, 0)
    send_t_z(0)
    loads[2].wait()
    loads[3].wait()
    send(("imgs",), xall.at[c], xall.at[c], sibling)
    send(("imgt",), xtall.at[c], xtall.at[c], sibling)

    def prepare(k):
        projected = jnp.dot(xall[k], w[...], preferred_element_type=f32)
        radius = jnp.sqrt(jnp.sum(projected * projected, axis=1, keepdims=True) + epsilon)
        u = projected / radius
        unit[k] = u
        rad[k] = radius
        low[k] = u.astype(bf16)
        v = xtall[k].astype(f32)
        teach[k] = (v / jnp.sqrt(jnp.sum(v * v, axis=1, keepdims=True) + epsilon)).astype(bf16)

    def turn():
        for k in range(2):
            flat = xall[k].astype(f32).T
            for yy in range(8):
                rows = [flat[zl * 192 + yy * 24 : zl * 192 + yy * 24 + 24] for zl in range(4)]
                xtp[yy, :, 128 * k : 128 * (k + 1)] = jnp.concatenate(rows, axis=0).astype(bf16)

    def hop(h):
        for pos in range(1, 8):
            if FLOW[pos][0] == h:
                arrive(("ty", pos), tb.at[0, pos])
                send_t_y(pos)
        if h <= 4:
            send_t_z(h)
        if h == 1:
            arrive(("sz", 1), sb.at[0, 1])
            send(("sz", 3), sb.at[0, 1], sb.at[0, 3], z_to[1])
            arrive(("sz", 2), sb.at[0, 2])
            send_s_y(0, 1)
        if h == 2:
            arrive(("sz", 3), sb.at[0, 3])
            send_s_y(0, 2)
        for part in range(3):
            for pos in range(1, 8):
                if FLOW[pos][0] + part == h:
                    arrive(("sy", pos, part), s_part(pos, part))
                    send_s_y(pos, part)
        if 0 <= h - 1 <= 4:
            group = h - 1
            arrive(("tz", 1, group), t_group(1, group))
            send(("tz", 3, group), t_group(1, group), t_group(3, group), z_to[1])
            arrive(("tz", 2, group), t_group(2, group))
        if 0 <= h - 2 <= 4:
            group = h - 2
            arrive(("tz", 3, group), t_group(3, group))

    def tile(group):
        start, count = GROUPS[group]
        n = count * 64
        rows = sb[start : start + count].reshape(n, 768)
        teach_rows = jnp.concatenate([tb[:, p].reshape(64, 1152) for p in range(start, start + count)], axis=0)
        low_all = low[...].reshape(256, 768)
        student = scales[0] * contract_last(rows, low_all) + biases[0]
        teacher = scales[1] * contract_last(teach_rows, teach[...].reshape(256, 1152)) + biases[1]
        target = 1.0 / (1.0 + jnp.exp(-teacher))
        small = jnp.exp(-jnp.abs(student))
        inverse = 1.0 / (1.0 + small)
        sig = jnp.where(student >= 0.0, inverse, small * inverse)
        loss = jnp.maximum(student, 0.0) + jnp.log1p(small) - target * student
        errors = (sig - target).astype(bf16)
        part = jnp.sum(loss, axis=0, keepdims=True)
        gradient = contract_first(errors, rows)
        if group == 0:
            lpart[...] = part
            grad[...] = gradient
        else:
            lpart[...] += part
            grad[...] += gradient
        term = jnp.dot(errors, low_all, preferred_element_type=f32).reshape(count, 4, 16, 768)
        town[start : start + count] = term[:, 0]
        for b in (1, 2, 3):
            zs[b - 1, start : start + count] = term[:, b].astype(bf16)

    def back_z(group):
        start, count = GROUPS[group]
        for b in (1, 2, 3):
            here = pl.ds(start, count)
            send(("gz", b, group), zs.at[b - 1, here], zr.at[b - 1, here], at(dz=-ZFLOW[b] * sgn))

    def back_y(group):
        start, count = GROUPS[group]
        here = pl.ds(start, count)
        for b in (1, 2, 3):
            arrive(("gz", b, group), zr.at[b - 1, here])
        total = town[start : start + count]
        for b in range(3):
            total = total + zr[b, start : start + count].astype(f32)
        town[start : start + count] = total
        for pos in range(start, start + count):
            if pos:
                steps, sign = FLOW[pos]
                send(("gy", pos), town.at[pos], yr.at[pos], at(dy=-steps * sign * sgn))

    loads[4].wait()
    hop(1)
    arrive(("imgs",), xall.at[1 - c])
    arrive(("imgt",), xtall.at[1 - c])
    prepare(0)
    hop(2)
    prepare(1)
    tile(0)
    back_z(0)
    hop(3)
    tile(1)
    back_z(1)
    back_y(0)
    hop(4)
    tile(2)
    back_z(2)
    back_y(1)
    hop(5)
    tile(3)
    back_z(3)
    back_y(2)
    turn()
    hop(6)
    tile(4)

    factor = loss_scale[0] * scales[0] / 8192.0
    g = grad[...] * factor
    u = unit[...].reshape(256, 768)
    step = (g - u * jnp.sum(g * u, axis=1, keepdims=True)) / rad[...].reshape(256, 1)
    for j in range(6):
        sfull[j] = step[:, 128 * j : 128 * (j + 1)]
    for k in range(2):
        lc[k] = jnp.broadcast_to(lpart[:, 128 * k : 128 * (k + 1)], (8, 128))
    send(("cs",), sfull.at[pl.ds(3 * (1 - c), 3)], crecv, sibling)
    send(("cl",), lc.at[1 - c], lc.at[2], sibling)
    back_z(4)
    back_y(3)

    arrive(("cs",), crecv)
    total = sfull[pl.ds(3 * c, 3)] + crecv[...]
    csum[...] = total
    sx[...] = total.astype(bf16)
    for r in (1, 2, 3):
        xto = lax.rem(x + r, 4)
        copy = message(("xs", r), sx.at[lax.rem(xto, 3)], xr.at[r - 1], at(dx=r))

        @pl.when(xto < 3)
        def _():
            copy.start()

    arrive(("cl",), lc.at[2])
    lx[...] = lc[c] + lc[2]
    for r in (1, 2, 3):
        send(("xl", r), lx, lxr.at[r - 1], at(dx=r))
    back_y(4)

    @pl.when(x < 3)
    def _():
        for r in (1, 2, 3):
            arrive(("xs", r), xr.at[r - 1])
        s = csum[x] + xr[0].astype(f32) + xr[1].astype(f32) + xr[2].astype(f32)
        high = s.astype(bf16)
        rest = (s - high.astype(f32)).astype(bf16)
        both = jnp.dot(xtp[...].reshape(768, 256), jnp.concatenate([high, rest], axis=1), preferred_element_type=f32)
        h = (both[:, :128] + both[:, 128:]).reshape(8, 96, 128)
        hsum[...] = h
        hb[...] = h.astype(bf16)
        for r in range(1, 8):
            message(("hy", r), hb.at[lax.rem(y + r, 8)], hr.at[r - 1], at(dy=r)).start()

    for r in (1, 2, 3):
        arrive(("xl", r), lxr.at[r - 1])
    lh[0] = lx[...] + lxr[0] + lxr[1] + lxr[2]
    send(("hl",), lh.at[0], lh.at[1], at(dz=4))

    for pos in range(1, 8):
        arrive(("gy", pos), yr.at[pos])
    tg = town[0]
    for pos in range(1, 8):
        tg = tg + yr[pos]
    tg = tg * factor
    tw = ts[...].astype(f32)
    tr = jnp.sqrt(jnp.sum(tw * tw, axis=1, keepdims=True) + epsilon)
    tu = tw / tr
    text_out[...] = (tg - tu * jnp.sum(tg * tu, axis=1, keepdims=True)) / tr

    @pl.when(x < 3)
    def _():
        for r in range(1, 8):
            arrive(("hy", r), hr.at[r - 1])
        total = hsum[y]
        for r in range(1, 8):
            total = total + hr[r - 1].astype(f32)
        zb[...] = total.reshape(4, 24, 128)
        for r in range(1, 8):
            message(("hz", r), zb.at[lax.rem(z + r, 4)], zrec.at[r - 1], at(dz=r)).start()

    arrive(("hl",), lh.at[1])
    loss_out[...] = (lh[0, 0:1] + lh[1, 0:1]) * (1.0 / 8192.0)

    mine = 3 * c + lax.rem(x, 3)

    @pl.when(x < 3)
    def _():
        for r in range(1, 8):
            arrive(("hz", r), zrec.at[r - 1])
        total = zb[lax.rem(z, 4)]
        for r in range(1, 8):
            total = total + zrec[r - 1]
        ag[mine] = total
        message(("agc",), ag.at[mine], ag.at[mine], sibling).start()
        for r in (1, 2, 3):
            for k in (0, 1):
                message(("agx", r, k), ag.at[mine], ag.at[mine], at(dx=r, core=c if k == 0 else 1 - c)).start()
        arrive(("agc",), ag.at[0])

    for r in (1, 2, 3):
        for k in (0, 1):

            @pl.when(lax.rem(x - r + 4, 4) < 3)
            def _(r=r, k=k):
                arrive(("agx", r, k), ag.at[0])

    for j in range(6):
        head_out[:, 128 * j : 128 * (j + 1)] = jnp.where(c == 0, ag[j, 0:12], ag[j, 12:24])

    for copy in sent:
        copy.wait_send()
    for r in (1, 2, 3):
        xto = lax.rem(x + r, 4)
        copy = message(("xs", r), sx.at[0], xr.at[r - 1], at(dx=r))

        @pl.when(xto < 3)
        def _():
            copy.wait_send()

    @pl.when(x < 3)
    def _():
        for r in range(1, 8):
            message(("hy", r), hb.at[0], hr.at[r - 1], at()).wait_send()
            message(("hz", r), zb.at[0], zrec.at[r - 1], at()).wait_send()
        message(("agc",), ag.at[0], ag.at[0], at()).wait_send()
        for r in (1, 2, 3):
            for k in (0, 1):
                message(("agx", r, k), ag.at[0], ag.at[0], at()).wait_send()


def shards(image_student, head_weight, text_student, image_teacher, text_teacher, logit_scales, logit_biases, loss_scale):
    vm = pltpu.VMEM
    scratch = [
        vm((2, 128, 768), bf16),
        vm((2, 128, 1152), bf16),
        vm((768, 768), bf16),
        vm((16, 768), bf16),
        vm((16, 1152), bf16),
        vm((8, 4, 16, 768), bf16),
        vm((4, 8, 16, 1152), bf16),
        vm((2, 128, 768), f32),
        vm((2, 128, 768), bf16),
        vm((2, 128, 1), f32),
        vm((2, 128, 1152), bf16),
        vm((8, 96, 256), bf16),
        vm((8, 128), f32),
        vm((8, 16, 768), f32),
        vm((3, 8, 16, 768), bf16),
        vm((3, 8, 16, 768), bf16),
        vm((8, 128), f32),
        vm((8, 16, 768), f32),
        vm((256, 768), f32),
        vm((6, 256, 128), f32),
        vm((3, 256, 128), f32),
        vm((3, 256, 128), f32),
        vm((3, 256, 128), bf16),
        vm((3, 256, 128), bf16),
        vm((8, 96, 128), f32),
        vm((8, 96, 128), bf16),
        vm((7, 96, 128), bf16),
        vm((4, 24, 128), f32),
        vm((7, 24, 128), f32),
        vm((6, 24, 128), f32),
        vm((1, 256), f32),
        vm((3, 8, 128), f32),
        vm((8, 128), f32),
        vm((3, 8, 128), f32),
        vm((2, 8, 128), f32),
        pltpu.SemaphoreType.DMA((5,)),
        pltpu.SemaphoreType.DMA((MESSAGES,)),
        pltpu.SemaphoreType.DMA((MESSAGES,)),
    ]
    any_spec = pl.BlockSpec(memory_space=pl.ANY)
    smem = pl.BlockSpec(memory_space=pltpu.SMEM)
    vmem = pl.BlockSpec(memory_space=pltpu.VMEM)
    head, text, loss = pl.pallas_call(
        kernel,
        out_shape=(
            jax.ShapeDtypeStruct((12, 768), f32),
            jax.ShapeDtypeStruct((16, 768), f32),
            jax.ShapeDtypeStruct((1, 128), f32),
        ),
        in_specs=[any_spec] * 5 + [smem] * 3,
        out_specs=(vmem, vmem, vmem),
        scratch_shapes=scratch,
        compiler_params=pltpu.CompilerParams(collective_id=0, has_side_effects=True, vmem_limit_bytes=48 * 1024 * 1024),
        name="distill",
    )(image_student, head_weight, text_student, image_teacher, text_teacher, logit_scales, logit_biases, loss_scale)
    return head, text, loss.reshape(128)


def solution(mesh):
    placed = (
        P("blk", None), P(), P(("blk", "txt"), None), P("blk", None), P(("blk", "txt"), None), P(), P(), P(),
    )
    return jax.shard_map(
        shards,
        mesh=mesh,
        in_specs=placed,
        out_specs=(P("blk", None), P(("blk", "txt"), None), P("blk")),
        check_vma=False,
    )
```

```python
import math

import jax
import jax.numpy as jnp
from jax import lax
from jax.experimental import pallas as pl
from jax.experimental.pallas import tpu as pltpu
from jax.sharding import PartitionSpec as P

epsilon = 1e-06
MESH = pl.DeviceIdType.MESH
f32 = jnp.float32
bf16 = jnp.bfloat16

FLOW = {1: (1, 1), 2: (1, -1), 3: (2, 1), 4: (2, -1), 5: (3, 1), 6: (3, -1), 7: (4, 1)}
NEXT = {1: 3, 2: 4, 3: 5, 4: 6, 5: 7}
GROUPS = [(0, 1), (1, 2), (3, 2), (5, 2), (7, 1)]
ZFLOW = {1: 1, 2: -1, 3: 2}


def contract_last(a, b):
    return lax.dot_general(a, b, (((1,), (1,)), ((), ())), preferred_element_type=f32)


def contract_first(a, b):
    return lax.dot_general(a, b, (((0,), (0,)), ((), ())), preferred_element_type=f32)


class Tags:
    def __init__(self):
        self.index = {}

    def __call__(self, key):
        return self.index.setdefault(key, len(self.index))


MESSAGES = 56
ROOM = 2048


def kernel(
    x_hbm, w_hbm, ts_hbm, xt_hbm, tt_hbm, scales_hbm, biases_hbm, loss_scale_hbm,
    head_out, text_out, loss_out,
    xall, xtall, w, ts, tt, sb, tb, unit, low, rad, teach, xtp,
    town, zs, zr, ysend, yr, grad, sfull, crecv, csum, sx, xr, hsum, hb, hr, zb, zrec, ag, lpart, lc, lx, lxr, lh,
    room, scales, biases, loss_scale, local_sem, send_sem, recv_sem,
):
    blk = lax.axis_index("blk")
    txt = lax.axis_index("txt")
    x = lax.rem(txt, 4)
    c = lax.rem(blk, 2)
    y = lax.rem(blk // 2, 8)
    z = (txt // 4) * 4 + blk // 16
    sgn = 2 * c - 1

    def at(dx=0, dy=0, dz=0, core=c):
        xx = lax.rem(x + dx + 8, 4)
        yy = lax.rem(y + dy + 16, 8)
        zz = lax.rem(z + dz + 16, 8)
        return {"blk": (lax.rem(zz, 4) * 8 + yy) * 2 + core, "txt": (zz // 4) * 4 + xx}

    barrier = pltpu.get_barrier_semaphore()
    partners = [at(core=1 - c)]
    partners += [at(dy=1), at(dy=-1), at(dz=1), at(dz=-1)]
    partners += [at(dz=-2 * sgn)] + [at(dx=r) for r in (1, 2, 3)]
    for partner in partners:
        pl.semaphore_signal(barrier, inc=1, device_id=partner, device_id_type=MESH)

    loads = [
        pltpu.make_async_copy(ts_hbm, ts, local_sem.at[0]),
        pltpu.make_async_copy(tt_hbm, tt, local_sem.at[1]),
        pltpu.make_async_copy(x_hbm, xall.at[c], local_sem.at[2]),
        pltpu.make_async_copy(xt_hbm, xtall.at[c], local_sem.at[3]),
        pltpu.make_async_copy(w_hbm, w, local_sem.at[4]),
        pltpu.make_async_copy(scales_hbm, scales, local_sem.at[5]),
        pltpu.make_async_copy(biases_hbm, biases, local_sem.at[6]),
        pltpu.make_async_copy(loss_scale_hbm, loss_scale, local_sem.at[7]),
    ]
    for copy in loads:
        copy.start()

    tags = Tags()
    left = {}

    def send(key, src, dst, device, lane=0):
        index = tags(key)
        assert index < MESSAGES
        pltpu.make_async_remote_copy(
            src, dst, send_sem.at[lane], recv_sem.at[index], device_id=device, device_id_type=MESH
        ).start()
        left[lane] = left.get(lane, 0) + math.prod(src.shape) * src.dtype.itemsize // 4096

    def arrive(key, dst):
        sem = recv_sem.at[tags(key)]
        pltpu.make_async_remote_copy(dst, dst, send_sem.at[0], sem, device_id=sibling, device_id_type=MESH).wait_recv()

    def gone(lane, units):
        view = room.at[pl.ds(0, units)]
        sem = send_sem.at[lane]
        pltpu.make_async_remote_copy(view, view, sem, recv_sem.at[0], device_id=sibling, device_id_type=MESH).wait_send()

    sibling = at(core=1 - c)

    loads[0].wait()
    loads[1].wait()
    t_wide = ts[...].astype(f32)
    t_rad = jnp.sqrt(jnp.sum(t_wide * t_wide, axis=1, keepdims=True) + epsilon)
    t_unit = t_wide / t_rad
    sb[0, 0] = t_unit.astype(bf16)
    q_wide = tt[...].astype(f32)
    tb[0, 0] = (q_wide / jnp.sqrt(jnp.sum(q_wide * q_wide, axis=1, keepdims=True) + epsilon)).astype(bf16)

    pl.semaphore_wait(barrier, len(partners))

    y_to = {1: at(dy=sgn), -1: at(dy=-sgn)}
    z_to = {1: at(dz=sgn), -1: at(dz=-sgn)}

    def s_part(pos, part):
        return sb.at[pos, pl.ds(0, 1)] if part == 0 else sb.at[pos, pl.ds(1, 2)] if part == 1 else sb.at[pos, pl.ds(3, 1)]

    def t_group(b, group):
        start, count = GROUPS[group]
        return tb.at[b, pl.ds(start, count)]

    def send_s_y(pos_from, part):
        targets = [(1, 1), (2, -1)] if pos_from == 0 else [(NEXT[pos_from], FLOW[pos_from][1])] if pos_from in NEXT else []
        for pos, sign in targets:
            send(("sy", pos, part), s_part(pos_from, part), s_part(pos, part), y_to[sign])

    def send_t_y(pos_from):
        targets = [(1, 1), (2, -1)] if pos_from == 0 else [(NEXT[pos_from], FLOW[pos_from][1])] if pos_from in NEXT else []
        for pos, sign in targets:
            send(("ty", pos), tb.at[0, pos_from], tb.at[0, pos], y_to[sign])

    def send_t_z(group):
        send(("tz", 1, group), t_group(0, group), t_group(1, group), z_to[1])
        send(("tz", 2, group), t_group(0, group), t_group(2, group), z_to[-1])

    send_t_y(0)
    send(("sz", 1), sb.at[0, 0], sb.at[0, 1], z_to[1])
    send(("sz", 1), sb.at[0, 0], sb.at[0, 2], z_to[-1])
    send(("sz", 3), sb.at[0, 0], sb.at[0, 3], at(dz=2 * sgn))
    send_s_y(0, 0)
    send_t_z(0)
    loads[2].wait()
    loads[3].wait()
    send("imgs", xall.at[c], xall.at[c], sibling)
    send("imgt", xtall.at[c], xtall.at[c], sibling)

    def prepare(k):
        projected = jnp.dot(xall[k], w[...], preferred_element_type=f32)
        radius = jnp.sqrt(jnp.sum(projected * projected, axis=1, keepdims=True) + epsilon)
        u = projected / radius
        unit[k] = u
        rad[k] = radius
        low[k] = u.astype(bf16)
        v = xtall[k].astype(f32)
        teach[k] = (v / jnp.sqrt(jnp.sum(v * v, axis=1, keepdims=True) + epsilon)).astype(bf16)

    def turn():
        for k in range(2):
            flat = xall[k].astype(f32).T
            for yy in range(8):
                rows = [flat[zl * 192 + yy * 24 : zl * 192 + yy * 24 + 24] for zl in range(4)]
                xtp[yy, :, 128 * k : 128 * (k + 1)] = jnp.concatenate(rows, axis=0).astype(bf16)

    def hop(h):
        for pos in range(1, 8):
            if FLOW[pos][0] == h:
                arrive(("ty", pos), tb.at[0, pos])
                send_t_y(pos)
        if h <= 4:
            send_t_z(h)
        if h == 1:
            arrive(("sz", 1), s_part(0, 1))
            send_s_y(0, 1)
        if h == 2:
            arrive(("sz", 3), sb.at[0, 3])
            send_s_y(0, 2)
        for part in range(3):
            for pos in range(1, 8):
                if FLOW[pos][0] + part == h:
                    arrive(("sy", pos, part), s_part(pos, part))
                    send_s_y(pos, part)
        if 0 <= h - 1 <= 4:
            group = h - 1
            arrive(("tz", 1, group), t_group(1, group))
            send(("tz", 2, group), t_group(1, group), t_group(3, group), z_to[1])

    def tile(group):
        start, count = GROUPS[group]
        arrive(("tz", 2, group), tb.at[pl.ds(2, 2), pl.ds(start, count)])
        n = count * 64
        rows = sb[start : start + count].reshape(n, 768)
        teach_rows = jnp.concatenate([tb[:, p].reshape(64, 1152) for p in range(start, start + count)], axis=0)
        low_all = low[...].reshape(256, 768)
        student = scales[0] * contract_last(rows, low_all) + biases[0]
        teacher = scales[1] * contract_last(teach_rows, teach[...].reshape(256, 1152)) + biases[1]
        target = 1.0 / (1.0 + jnp.exp(-teacher))
        small = jnp.exp(-jnp.abs(student))
        inverse = 1.0 / (1.0 + small)
        sig = jnp.where(student >= 0.0, inverse, small * inverse)
        loss = jnp.maximum(student, 0.0) + jnp.log1p(small) - target * student
        errors = (sig - target).astype(bf16)
        part = jnp.sum(loss, axis=0, keepdims=True)
        gradient = contract_first(errors, rows)
        if group == 0:
            lpart[...] = part
            grad[...] = gradient
        else:
            lpart[...] += part
            grad[...] += gradient
        term = jnp.dot(errors, low_all, preferred_element_type=f32).reshape(count, 4, 16, 768)
        town[start : start + count] = term[:, 0]
        for b in (1, 2, 3):
            zs[b - 1, start : start + count] = term[:, b].astype(bf16)

    def back_z():
        for b in (3, 1, 2):
            send("gz", zs.at[b - 1], zr.at[b - 1], at(dz=-ZFLOW[b] * sgn))

    def sum_z():
        arrive("gz", zr)
        total = town[...]
        for b in range(3):
            total = total + zr[b].astype(f32)
        town[...] = total
        ysend[...] = total.astype(bf16)

    def back_y(pos):
        steps, sign = FLOW[pos]
        send("gy", ysend.at[pos], yr.at[pos - 1], at(dy=-steps * sign * sgn))

    for copy in loads[4:]:
        copy.wait()
    hop(1)
    arrive("imgs", xall.at[1 - c])
    arrive("imgt", xtall.at[1 - c])
    prepare(0)
    hop(2)
    prepare(1)
    hop(3)
    tile(0)
    hop(4)
    tile(1)
    hop(5)
    tile(2)
    turn()
    tile(3)
    hop(6)
    tile(4)

    factor = loss_scale[0] * scales[0] / 8192.0
    g = grad[...] * factor
    u = unit[...].reshape(256, 768)
    step = (g - u * jnp.sum(g * u, axis=1, keepdims=True)) / rad[...].reshape(256, 1)
    for j in range(6):
        sfull[j] = step[:, 128 * j : 128 * (j + 1)]
    for k in range(2):
        lc[k] = jnp.broadcast_to(lpart[:, 128 * k : 128 * (k + 1)], (8, 128))
    send("cs", sfull.at[pl.ds(3 * (1 - c), 3)], crecv, sibling)
    send("cl", lc.at[1 - c], lc.at[2], sibling)
    back_z()

    arrive("cs", crecv)
    total = sfull[pl.ds(3 * c, 3)] + crecv[...]
    csum[...] = total
    sx[...] = total.astype(bf16)
    for r in (1, 2, 3):
        xto = lax.rem(x + r, 4)

        @pl.when(xto < 3)
        def _():
            send("xs", sx.at[lax.rem(xto, 3)], xr.at[r - 1], at(dx=r), lane=r)

    arrive("cl", lc.at[2])
    lx[...] = lc[c] + lc[2]
    for r in (1, 2, 3):
        send("xl", lx, lxr.at[r - 1], at(dx=r))

    @pl.when(x < 3)
    def _():
        arrive("xs", xr)
        s = csum[x] + xr[0].astype(f32) + xr[1].astype(f32) + xr[2].astype(f32)
        high = s.astype(bf16)
        rest = (s - high.astype(f32)).astype(bf16)
        both = jnp.dot(xtp[...].reshape(768, 256), jnp.concatenate([high, rest], axis=1), preferred_element_type=f32)
        h = (both[:, :128] + both[:, 128:]).reshape(8, 96, 128)
        hsum[...] = h
        hb[...] = h.astype(bf16)
        for r in range(1, 8):
            send("hy", hb.at[lax.rem(y + r, 8)], hr.at[r - 1], at(dy=r), lane=4)

    arrive("xl", lxr)
    lh[0] = lx[...] + lxr[0] + lxr[1] + lxr[2]
    send("hl", lh.at[0], lh.at[1], at(dz=4))
    sum_z()

    @pl.when(x < 3)
    def _():
        arrive("hy", hr)
        total = hsum[y]
        for r in range(1, 8):
            total = total + hr[r - 1].astype(f32)
        zb[...] = total.reshape(4, 24, 128)
        for r in range(1, 8):
            send("hz", zb.at[lax.rem(z + r, 4)], zrec.at[r - 1], at(dz=r), lane=4)

    for pos in range(7, 0, -1):
        back_y(pos)
    arrive("hl", lh.at[1])
    loss_out[...] = (lh[0, 0:1] + lh[1, 0:1]) * (1.0 / 8192.0)

    mine = 3 * c + lax.rem(x, 3)

    @pl.when(x < 3)
    def _():
        arrive("hz", zrec)
        total = zb[lax.rem(z, 4)]
        for r in range(1, 8):
            total = total + zrec[r - 1]
        ag[mine] = total
        send("ag", ag.at[mine], ag.at[mine], sibling, lane=4)
        for r in (1, 2, 3):
            for k in (0, 1):
                send("ag", ag.at[mine], ag.at[mine], at(dx=r, core=c if k == 0 else 1 - c), lane=4)

    arrive("gy", yr)
    tg = town[0]
    for pos in range(1, 8):
        tg = tg + yr[pos - 1].astype(f32)
    tg = tg * factor
    tw = ts[...].astype(f32)
    tr = jnp.sqrt(jnp.sum(tw * tw, axis=1, keepdims=True) + epsilon)
    tu = tw / tr
    text_out[...] = (tg - tu * jnp.sum(tg * tu, axis=1, keepdims=True)) / tr

    @pl.when(x < 3)
    def _():
        arrive("ag", ag.at[pl.ds(0, 5)])

    @pl.when(x == 3)
    def _():
        arrive("ag", ag)

    for j in range(6):
        head_out[:, 128 * j : 128 * (j + 1)] = jnp.where(c == 0, ag[j, 0:12], ag[j, 12:24])

    gone(0, left[0])
    for r in (1, 2, 3):

        @pl.when(lax.rem(x + r, 4) < 3)
        def _():
            gone(r, left[r])

    @pl.when(x < 3)
    def _():
        gone(4, left[4])


def shards(image_student, head_weight, text_student, image_teacher, text_teacher, logit_scales, logit_biases, loss_scale):
    vm = pltpu.VMEM
    scratch = [
        vm((2, 128, 768), bf16),
        vm((2, 128, 1152), bf16),
        vm((768, 768), bf16),
        vm((16, 768), bf16),
        vm((16, 1152), bf16),
        vm((8, 4, 16, 768), bf16),
        vm((4, 8, 16, 1152), bf16),
        vm((2, 128, 768), f32),
        vm((2, 128, 768), bf16),
        vm((2, 128, 1), f32),
        vm((2, 128, 1152), bf16),
        vm((8, 96, 256), bf16),
        vm((8, 16, 768), f32),
        vm((3, 8, 16, 768), bf16),
        vm((3, 8, 16, 768), bf16),
        vm((8, 16, 768), bf16),
        vm((7, 16, 768), bf16),
        vm((256, 768), f32),
        vm((6, 256, 128), f32),
        vm((3, 256, 128), f32),
        vm((3, 256, 128), f32),
        vm((3, 256, 128), bf16),
        vm((3, 256, 128), bf16),
        vm((8, 96, 128), f32),
        vm((8, 96, 128), bf16),
        vm((7, 96, 128), bf16),
        vm((4, 24, 128), f32),
        vm((7, 24, 128), f32),
        vm((6, 24, 128), f32),
        vm((1, 256), f32),
        vm((3, 8, 128), f32),
        vm((8, 128), f32),
        vm((3, 8, 128), f32),
        vm((2, 8, 128), f32),
        vm((ROOM, 8, 128), f32),
        pltpu.SMEM((2,), f32),
        pltpu.SMEM((2,), f32),
        pltpu.SMEM((1,), f32),
        pltpu.SemaphoreType.DMA((8,)),
        pltpu.SemaphoreType.DMA((5,)),
        pltpu.SemaphoreType.DMA((MESSAGES,)),
    ]
    hbm = pl.BlockSpec(memory_space=pltpu.HBM)
    vmem = pl.BlockSpec(memory_space=pltpu.VMEM)
    head, text, loss = pl.pallas_call(
        kernel,
        out_shape=(
            pltpu.VMEM((12, 768), f32),
            pltpu.VMEM((16, 768), f32),
            pltpu.VMEM((1, 128), f32),
        ),
        in_specs=[hbm] * 8,
        out_specs=(vmem, vmem, vmem),
        scratch_shapes=scratch,
        compiler_params=pltpu.CompilerParams(collective_id=0, has_side_effects=True, vmem_limit_bytes=60 * 1024 * 1024),
        name="distill",
    )(image_student, head_weight, text_student, image_teacher, text_teacher, logit_scales, logit_biases, loss_scale)
    return head, text, loss.reshape(128)


def solution(mesh):
    placed = (
        P("blk", None), P(), P(("blk", "txt"), None), P("blk", None), P(("blk", "txt"), None), P(), P(), P(),
    )
    return jax.shard_map(
        shards,
        mesh=mesh,
        in_specs=placed,
        out_specs=(P("blk", None), P(("blk", "txt"), None), P("blk")),
        check_vma=False,
    )
```

```python
import math

import jax
import jax.numpy as jnp
from jax import lax
from jax.experimental import pallas as pl
from jax.experimental.pallas import tpu as pltpu
from jax.sharding import PartitionSpec as P

epsilon = 1e-06
MESH = pl.DeviceIdType.MESH
f32 = jnp.float32
bf16 = jnp.bfloat16

FLOW = {1: (1, 1), 2: (1, -1), 3: (2, 1), 4: (2, -1), 5: (3, 1), 6: (3, -1), 7: (4, 1)}
BEFORE = {1: 0, 2: 0, 3: 1, 4: 2, 5: 3, 6: 4, 7: 5}
GROUPS = [(0, 1), (1, 2), (3, 2), (5, 2), (7, 1)]
ZFLOW = {1: 1, 2: -1, 3: 2}
ORDER = [
    ("ty", 1), ("ty", 2), ("sz", 1), ("sz", 2), ("sz", 3), ("sy", 1, 0), ("sy", 2, 0), ("tz", 1, 0), ("tz", 2, 0),
    ("images",), ("prepare", 0), ("prepare", 1), ("turn",),
    ("ty", 3), ("ty", 4), ("sy", 1, 1), ("sy", 2, 1), ("sy", 3, 0), ("tz", 1, 1), ("sy", 4, 0), ("tz", 2, 1), ("tz", 3, 0),
    ("sy", 1, 2), ("sy", 2, 2), ("ty", 5), ("sy", 5, 0), ("ty", 6), ("tz", 1, 2), ("tz", 2, 2), ("tz", 3, 1), ("sy", 6, 0),
    ("tile", 0),
    ("sy", 3, 1), ("sy", 3, 2), ("ty", 7), ("sy", 4, 1), ("sy", 4, 2), ("sy", 7, 0), ("tz", 1, 3), ("tz", 2, 3), ("tz", 3, 2),
    ("sy", 5, 2),
    ("tile", 1),
    ("sy", 5, 1), ("tz", 1, 4), ("sy", 6, 1), ("tz", 2, 4), ("tz", 3, 3), ("sy", 6, 2), ("sy", 7, 2),
    ("tile", 2),
    ("tz", 3, 4), ("sy", 7, 1),
    ("tile", 3),
]


def contract_last(a, b):
    return lax.dot_general(a, b, (((1,), (1,)), ((), ())), preferred_element_type=f32)


def contract_first(a, b):
    return lax.dot_general(a, b, (((0,), (0,)), ((), ())), preferred_element_type=f32)


class Tags:
    def __init__(self):
        self.index = {}

    def __call__(self, key):
        return self.index.setdefault(key, len(self.index))


MESSAGES = 56
ROOM = 2048


def kernel(
    x_hbm, w_hbm, ts_hbm, xt_hbm, tt_hbm, scales_hbm, biases_hbm, loss_scale_hbm,
    head_out, text_out, loss_out,
    xall, xtall, w, ts, tt, sb, tb, unit, low, rad, teach, xtp,
    town, zs, zr, ysend, yr, grad, csend, crecv, csum, sx, xr, hsum, hb, hr, zb, zrec, agsend, ag, lpart, lc, lx, lxr, lh,
    room, scales, biases, loss_scale, local_sem, send_sem, recv_sem,
):
    blk = lax.axis_index("blk")
    txt = lax.axis_index("txt")
    x = lax.rem(txt, 4)
    c = lax.rem(blk, 2)
    y = lax.rem(blk // 2, 8)
    z = (txt // 4) * 4 + blk // 16
    sgn = 2 * c - 1

    def at(dx=0, dy=0, dz=0, core=c):
        xx = lax.rem(x + dx + 8, 4)
        yy = lax.rem(y + dy + 16, 8)
        zz = lax.rem(z + dz + 16, 8)
        return {"blk": (lax.rem(zz, 4) * 8 + yy) * 2 + core, "txt": (zz // 4) * 4 + xx}

    barrier = pltpu.get_barrier_semaphore()
    partners = [at(core=1 - c)]
    partners += [at(dy=1), at(dy=-1), at(dz=1), at(dz=-1)]
    partners += [at(dz=-2 * sgn)] + [at(dx=r) for r in (1, 2, 3)]
    for partner in partners:
        pl.semaphore_signal(barrier, inc=1, device_id=partner, device_id_type=MESH)

    loads = [
        pltpu.make_async_copy(ts_hbm, ts, local_sem.at[0]),
        pltpu.make_async_copy(tt_hbm, tt, local_sem.at[1]),
        pltpu.make_async_copy(x_hbm, xall.at[c], local_sem.at[2]),
        pltpu.make_async_copy(xt_hbm, xtall.at[c], local_sem.at[3]),
        pltpu.make_async_copy(w_hbm, w, local_sem.at[4]),
        pltpu.make_async_copy(scales_hbm, scales, local_sem.at[5]),
        pltpu.make_async_copy(biases_hbm, biases, local_sem.at[6]),
        pltpu.make_async_copy(loss_scale_hbm, loss_scale, local_sem.at[7]),
    ]
    for copy in loads:
        copy.start()

    tags = Tags()
    left = {}

    def send(key, src, dst, device, lane=0):
        index = tags(key)
        assert index < MESSAGES
        pltpu.make_async_remote_copy(
            src, dst, send_sem.at[lane], recv_sem.at[index], device_id=device, device_id_type=MESH
        ).start()
        left[lane] = left.get(lane, 0) + math.prod(src.shape) * src.dtype.itemsize // 4096

    def arrive(key, dst):
        sem = recv_sem.at[tags(key)]
        pltpu.make_async_remote_copy(dst, dst, send_sem.at[0], sem, device_id=sibling, device_id_type=MESH).wait_recv()

    def gone(lane, units):
        view = room.at[pl.ds(0, units)]
        sem = send_sem.at[lane]
        pltpu.make_async_remote_copy(view, view, sem, recv_sem.at[0], device_id=sibling, device_id_type=MESH).wait_send()

    sibling = at(core=1 - c)

    loads[0].wait()
    loads[1].wait()
    t_wide = ts[...].astype(f32)
    t_rad = jnp.sqrt(jnp.sum(t_wide * t_wide, axis=1, keepdims=True) + epsilon)
    t_unit = t_wide / t_rad
    sb[0, 0] = t_unit.astype(bf16)
    q_wide = tt[...].astype(f32)
    tb[0, 0] = (q_wide / jnp.sqrt(jnp.sum(q_wide * q_wide, axis=1, keepdims=True) + epsilon)).astype(bf16)

    pl.semaphore_wait(barrier, len(partners))

    y_to = {1: at(dy=sgn), -1: at(dy=-sgn)}
    z_to = {1: at(dz=sgn), -1: at(dz=-sgn)}

    def s_part(pos, part):
        return sb.at[pos, pl.ds(0, 1)] if part == 0 else sb.at[pos, pl.ds(1, 2)] if part == 1 else sb.at[pos, pl.ds(3, 1)]

    def t_group(b, group):
        start, count = GROUPS[group]
        return tb.at[b, pl.ds(start, count)]

    def gather_message(key):
        kind = key[0]
        if kind == "ty":
            pos = key[1]
            return [("ty", BEFORE[pos])], tb.at[0, BEFORE[pos]], tb.at[0, pos], y_to[FLOW[pos][1]]
        if kind == "sy":
            pos, part = key[1:]
            parents = [("sy", BEFORE[pos], part)] if BEFORE[pos] else [[], [("sz", 1)], [("sz", 3)]][part]
            return parents, s_part(BEFORE[pos], part), s_part(pos, part), y_to[FLOW[pos][1]]
        if kind == "sz":
            b = key[1]
            return [], sb.at[0, 0], sb.at[0, b], at(dz=ZFLOW[b] * sgn)
        b, group = key[1:]
        start, count = GROUPS[group]
        if b == 3:
            return [("tz", 1, group)], t_group(1, group), t_group(3, group), z_to[1]
        return [("ty", pos) for pos in range(start, start + count)], t_group(0, group), t_group(b, group), z_to[ZFLOW[b]]

    waited = {("ty", 0)}

    def need(key):
        if key in waited:
            return
        waited.add(key)
        kind = key[0]
        if kind == "ty":
            arrive(key, tb.at[0, key[1]])
        elif kind == "sy":
            arrive(key, s_part(key[1], key[2]))
        elif kind == "sz":
            arrive(key, s_part(0, 1) if key[1] == 1 else s_part(0, 2))
        elif key[1] == 1:
            arrive(key, t_group(1, key[2]))
        else:
            start, count = GROUPS[key[2]]
            arrive(key, tb.at[pl.ds(2, 2), pl.ds(start, count)])

    def pass_on(key):
        parents, src, dst, device = gather_message(key)
        for parent in parents:
            need(parent)
        if key[0] == "tz" and key[1] == 3:
            key = ("tz", 2, key[2])
        if key == ("sz", 2):
            key = ("sz", 1)
        send(key, src, dst, device)

    def prepare(k):
        projected = jnp.dot(xall[k], w[...], preferred_element_type=f32)
        radius = jnp.sqrt(jnp.sum(projected * projected, axis=1, keepdims=True) + epsilon)
        u = projected / radius
        here = pl.ds(128 * k, 128)
        for j in range(6):
            unit[j, here] = u[:, 128 * j : 128 * (j + 1)]
        rad[here] = 1.0 / radius
        low[k] = u.astype(bf16)
        v = xtall[k].astype(f32)
        teach[k] = (v / jnp.sqrt(jnp.sum(v * v, axis=1, keepdims=True) + epsilon)).astype(bf16)

    def turn():
        for k in range(2):
            flat = xall[k].astype(f32).T
            for yy in range(8):
                rows = [flat[zl * 192 + yy * 24 : zl * 192 + yy * 24 + 24] for zl in range(4)]
                xtp[yy, :, 128 * k : 128 * (k + 1)] = jnp.concatenate(rows, axis=0).astype(bf16)

    def tile(group):
        start, count = GROUPS[group]
        for pos in range(start, start + count):
            need(("ty", pos))
            for part in range(3):
                if pos:
                    need(("sy", pos, part))
        for key in [("sz", 1), ("sz", 3), ("tz", 1, group), ("tz", 2, group)]:
            need(key)
        n = count * 64
        rows = sb[start : start + count].reshape(n, 768)
        teach_rows = jnp.concatenate([tb[:, p].reshape(64, 1152) for p in range(start, start + count)], axis=0)
        low_all = low[...].reshape(256, 768)
        student = scales[0] * contract_last(rows, low_all) + biases[0]
        teacher = scales[1] * contract_last(teach_rows, teach[...].reshape(256, 1152)) + biases[1]
        target = 1.0 / (1.0 + jnp.exp(-teacher))
        small = jnp.exp(-jnp.abs(student))
        inverse = 1.0 / (1.0 + small)
        sig = jnp.where(student >= 0.0, inverse, small * inverse)
        loss = jnp.maximum(student, 0.0) + jnp.log1p(small) - target * student
        errors = (sig - target).astype(bf16)
        part = jnp.sum(loss, axis=0, keepdims=True)
        gradient = contract_first(errors, rows)
        if group == 0:
            lpart[...] = part
        else:
            lpart[...] += part
        for j in range(6):
            columns = gradient[:, 128 * j : 128 * (j + 1)]
            grad[j] = columns if group == 0 else grad[j] + columns
        return errors

    def terms(group, errors):
        start, count = GROUPS[group]
        term = jnp.dot(errors, low[...].reshape(256, 768), preferred_element_type=f32).reshape(count, 4, 16, 768)
        town[start : start + count] = term[:, 0]
        for b in (1, 2, 3):
            zs[b - 1, start : start + count] = term[:, b].astype(bf16)

    def back_z():
        for b in (3, 1, 2):
            send("gz", zs.at[b - 1], zr.at[b - 1], at(dz=-ZFLOW[b] * sgn))

    def sum_z():
        arrive("gz", zr)
        total = town[...]
        for b in range(3):
            total = total + zr[b].astype(f32)
        town[...] = total
        ysend[...] = total.astype(bf16)

    def back_y(pos):
        steps, sign = FLOW[pos]
        send("gy", ysend.at[pos], yr.at[pos - 1], at(dy=-steps * sign * sgn))

    for action in ORDER:
        kind = action[0]
        if kind == "images":
            loads[2].wait()
            loads[3].wait()
            send("imgs", xall.at[c], xall.at[c], sibling)
            send("imgt", xtall.at[c], xtall.at[c], sibling)
            for copy in loads[4:]:
                copy.wait()
        elif kind == "prepare":
            if action[1] == 1:
                arrive("imgs", xall.at[1 - c])
                arrive("imgt", xtall.at[1 - c])
            prepare(c if action[1] == 0 else 1 - c)
        elif kind == "turn":
            turn()
        elif kind == "tile":
            terms(action[1], tile(action[1]))
        else:
            pass_on(action)
    last_errors = tile(4)

    factor = loss_scale[0] * scales[0] / 8192.0
    radial = grad[0] * unit[0]
    for j in range(1, 6):
        radial = radial + grad[j] * unit[j]
    radial = jnp.sum(radial, axis=1, keepdims=True)
    over = rad[...] * factor

    def step(j):
        return (grad[j] - unit[j] * radial) * over

    for j in range(3):
        csend[j] = step(3 * (1 - c) + j)
        send(("cs", j), csend.at[j], crecv.at[j], sibling)
    for j in range(3):
        csum[j] = step(3 * c + j)
    for k in range(2):
        lc[k] = jnp.broadcast_to(lpart[:, 128 * k : 128 * (k + 1)], (8, 128))
    send("cl", lc.at[1 - c], lc.at[2], sibling)

    for j in range(3):
        arrive(("cs", j), crecv.at[j])
        total = csum[j] + crecv[j]

        @pl.when(x == j)
        def _():
            csum[j] = total

        @pl.when(x != j)
        def _():
            sx[j] = total.astype(bf16)
            send("xs", sx.at[j], xr.at[lax.rem(j - x + 4, 4) - 1], at(dx=j - x), lane=1 + j)

    terms(4, last_errors)
    back_z()
    arrive("cl", lc.at[2])
    lx[...] = lc[c] + lc[2]
    for r in (2, 1, 3):
        send("xl", lx, lxr.at[r - 1], at(dx=r))

    @pl.when(x < 3)
    def _():
        arrive("xs", xr)
        s = csum[x] + xr[0].astype(f32) + xr[1].astype(f32) + xr[2].astype(f32)
        high = s.astype(bf16)
        both = jnp.concatenate([high, (s - high.astype(f32)).astype(bf16)], axis=1)
        for half in ((4, 3, 5, 2), (6, 1, 7, 0)):
            turned = jnp.concatenate([xtp[lax.rem(y + r, 8)] for r in half], axis=0)
            product = jnp.dot(turned, both, preferred_element_type=f32)
            h = (product[:, :128] + product[:, 128:]).reshape(4, 96, 128)
            for place, r in enumerate(half):
                if r == 0:
                    hsum[...] = h[place]
                else:
                    hb[r - 1] = h[place].astype(bf16)
                    send("hy", hb.at[r - 1], hr.at[r - 1], at(dy=r), lane=4)

    arrive("xl", lxr)
    lh[0] = lx[...] + lxr[0] + lxr[1] + lxr[2]
    send("hl", lh.at[0], lh.at[1], at(dz=4))
    sum_z()

    @pl.when(x < 3)
    def _():
        arrive("hy", hr)
        total = hsum[...]
        for r in range(1, 8):
            total = total + hr[r - 1].astype(f32)
        zb[...] = total.reshape(4, 24, 128)
        for r in (4, 3, 5, 2, 6, 1, 7):
            send("hz", zb.at[lax.rem(z + r, 4)], zrec.at[r - 1], at(dz=r), lane=4)

    for pos in range(7, 0, -1):
        back_y(pos)
    arrive("hl", lh.at[1])
    loss_out[...] = (lh[0, 0:1] + lh[1, 0:1]) * (1.0 / 8192.0)

    mine = 3 * c + lax.rem(x, 3)

    @pl.when(x < 3)
    def _():
        arrive("hz", zrec)
        total = zb[lax.rem(z, 4)]
        for r in range(1, 8):
            total = total + zrec[r - 1]
        agsend[0] = total[0:16]
        agsend[1] = total[8:24]
        ag[mine] = agsend[c]
        for r in (2, 1, 3):
            for k in (0, 1):
                send("ag", agsend.at[k], ag.at[mine], at(dx=r, core=k), lane=4)
        send("ag", agsend.at[1 - c], ag.at[mine], sibling, lane=4)

    arrive("gy", yr)
    tg = town[0]
    for pos in range(1, 8):
        tg = tg + yr[pos - 1].astype(f32)
    tg = tg * factor
    tw = ts[...].astype(f32)
    tr = jnp.sqrt(jnp.sum(tw * tw, axis=1, keepdims=True) + epsilon)
    tu = tw / tr
    text_out[...] = (tg - tu * jnp.sum(tg * tu, axis=1, keepdims=True)) / tr

    @pl.when(x < 3)
    def _():
        arrive("ag", ag.at[pl.ds(0, 5)])

    @pl.when(x == 3)
    def _():
        arrive("ag", ag)

    for j in range(6):
        head_out[:, 128 * j : 128 * (j + 1)] = jnp.where(c == 0, ag[j, 0:12], ag[j, 4:16])

    gone(0, left[0])
    for j in range(3):

        @pl.when(x != j)
        def _():
            gone(1 + j, left[1 + j])

    @pl.when(x < 3)
    def _():
        gone(4, left[4])


def shards(image_student, head_weight, text_student, image_teacher, text_teacher, logit_scales, logit_biases, loss_scale):
    vm = pltpu.VMEM
    scratch = [
        vm((2, 128, 768), bf16),
        vm((2, 128, 1152), bf16),
        vm((768, 768), bf16),
        vm((16, 768), bf16),
        vm((16, 1152), bf16),
        vm((8, 4, 16, 768), bf16),
        vm((4, 8, 16, 1152), bf16),
        vm((6, 256, 128), f32),
        vm((2, 128, 768), bf16),
        vm((256, 1), f32),
        vm((2, 128, 1152), bf16),
        vm((8, 96, 256), bf16),
        vm((8, 16, 768), f32),
        vm((3, 8, 16, 768), bf16),
        vm((3, 8, 16, 768), bf16),
        vm((8, 16, 768), bf16),
        vm((7, 16, 768), bf16),
        vm((6, 256, 128), f32),
        vm((3, 256, 128), f32),
        vm((3, 256, 128), f32),
        vm((3, 256, 128), f32),
        vm((3, 256, 128), bf16),
        vm((3, 256, 128), bf16),
        vm((96, 128), f32),
        vm((7, 96, 128), bf16),
        vm((7, 96, 128), bf16),
        vm((4, 24, 128), f32),
        vm((7, 24, 128), f32),
        vm((2, 16, 128), f32),
        vm((6, 16, 128), f32),
        vm((1, 256), f32),
        vm((3, 8, 128), f32),
        vm((8, 128), f32),
        vm((3, 8, 128), f32),
        vm((2, 8, 128), f32),
        vm((ROOM, 8, 128), f32),
        pltpu.SMEM((2,), f32),
        pltpu.SMEM((2,), f32),
        pltpu.SMEM((1,), f32),
        pltpu.SemaphoreType.DMA((8,)),
        pltpu.SemaphoreType.DMA((5,)),
        pltpu.SemaphoreType.DMA((MESSAGES,)),
    ]
    hbm = pl.BlockSpec(memory_space=pltpu.HBM)
    vmem = pl.BlockSpec(memory_space=pltpu.VMEM)
    head, text, loss = pl.pallas_call(
        kernel,
        out_shape=(
            pltpu.VMEM((12, 768), f32),
            pltpu.VMEM((16, 768), f32),
            pltpu.VMEM((1, 128), f32),
        ),
        in_specs=[hbm] * 8,
        out_specs=(vmem, vmem, vmem),
        scratch_shapes=scratch,
        compiler_params=pltpu.CompilerParams(collective_id=0, has_side_effects=True, vmem_limit_bytes=60 * 1024 * 1024),
        name="distill",
    )(image_student, head_weight, text_student, image_teacher, text_teacher, logit_scales, logit_biases, loss_scale)
    return head, text, loss.reshape(128)


def solution(mesh):
    placed = (
        P("blk", None), P(), P(("blk", "txt"), None), P("blk", None), P(("blk", "txt"), None), P(), P(), P(),
    )
    return jax.shard_map(
        shards,
        mesh=mesh,
        in_specs=placed,
        out_specs=(P("blk", None), P(("blk", "txt"), None), P("blk")),
        check_vma=False,
    )
```

```python
import math

import jax
import jax.numpy as jnp
from jax import lax
from jax.experimental import pallas as pl
from jax.experimental.pallas import tpu as pltpu
from jax.sharding import PartitionSpec as P

epsilon = 1e-06
MESH = pl.DeviceIdType.MESH
f32 = jnp.float32
bf16 = jnp.bfloat16

FLOW = {1: (1, 1), 2: (1, -1), 3: (2, 1), 4: (2, -1), 5: (3, 1), 6: (3, -1), 7: (4, 1)}
T_TREE = {1: (0, 1), 2: (0, 1), 3: (0, 2), 4: (0, 2), 5: (1, 2), 6: (4, 1), 7: (5, 1)}
S_TREES = [
    {1: (0, 1), 2: (0, 1), 3: (1, 1), 4: (2, 1), 5: (3, 1), 6: (4, 1), 7: (3, 2)},
    {1: (0, 1), 2: (0, 1), 3: (0, 2), 4: (0, 2), 5: (1, 2), 6: (2, 2), 7: (3, 2)},
]
LONG = (0, 3)
GROUPS = [(0, 1), (1, 2), (3, 2), (5, 2), (7, 1)]
ZFLOW = {1: 1, 2: -1, 3: 2}
ORDER = [
    ("ty", 1), ("sz", 1), ("sz", 2), ("ty", 4), ("ty", 3), ("ty", 2), ("sz", 3), ("tz", 3, 0), ("tz", 1, 0), ("tz", 2, 0),
    ("images",), ("prepare", 0), ("prepare", 1), ("ty", 5), ("turn",), ("sy", 1, 0), ("sy", 2, 0), ("tz", 1, 1),
    ("tz", 2, 1), ("ty", 6), ("tz", 1, 2), ("sy", 3, 1), ("sy", 1, 1), ("sy", 2, 1), ("tz", 2, 2), ("sy", 4, 1), ("tile", 0),
    ("ty", 7), ("sy", 3, 0), ("sy", 4, 0), ("tz", 3, 1), ("tz", 3, 3), ("tz", 1, 3), ("tz", 2, 3), ("sy", 5, 1),
    ("sy", 6, 1), ("tz", 3, 2), ("tz", 1, 4), ("sy", 7, 1), ("tz", 2, 4), ("sy", 7, 0), ("sy", 5, 0), ("sy", 6, 0),
    ("tile", 1), ("tz", 3, 4), ("tile", 2), ("tile", 3),
]


def contract_last(a, b):
    return lax.dot_general(a, b, (((1,), (1,)), ((), ())), preferred_element_type=f32)


def contract_first(a, b):
    return lax.dot_general(a, b, (((0,), (0,)), ((), ())), preferred_element_type=f32)


class Tags:
    def __init__(self):
        self.index = {}

    def __call__(self, key):
        return self.index.setdefault(key, len(self.index))


MESSAGES = 56
ROOM = 2048


def kernel(
    x_hbm, w_hbm, ts_hbm, xt_hbm, tt_hbm, scales_hbm, biases_hbm, loss_scale_hbm,
    head_out, text_out, loss_out,
    xall, xtall, w, ts, tt, sb, tb, unit, low, rad, teach, xtp,
    kept, town, zs, zr, ysend, yr, grad, csend, crecv, csum, sx, xr, hsum, hb, hr, zb, zrec, agsend, ag, lpart, lc, lx, lxr, lh,
    room, scales, biases, loss_scale, local_sem, send_sem, recv_sem,
):
    blk = lax.axis_index("blk")
    txt = lax.axis_index("txt")
    x = lax.rem(txt, 4)
    c = lax.rem(blk, 2)
    y = lax.rem(blk // 2, 8)
    z = (txt // 4) * 4 + blk // 16
    sgn = 2 * c - 1

    def at(dx=0, dy=0, dz=0, core=c):
        xx = lax.rem(x + dx + 8, 4)
        yy = lax.rem(y + dy + 16, 8)
        zz = lax.rem(z + dz + 16, 8)
        return {"blk": (lax.rem(zz, 4) * 8 + yy) * 2 + core, "txt": (zz // 4) * 4 + xx}

    loads = [
        pltpu.make_async_copy(ts_hbm, ts, local_sem.at[0]),
        pltpu.make_async_copy(tt_hbm, tt, local_sem.at[1]),
        pltpu.make_async_copy(x_hbm, xall.at[c], local_sem.at[2]),
        pltpu.make_async_copy(xt_hbm, xtall.at[c], local_sem.at[3]),
        pltpu.make_async_copy(w_hbm, w, local_sem.at[4]),
        pltpu.make_async_copy(scales_hbm, scales, local_sem.at[5]),
        pltpu.make_async_copy(biases_hbm, biases, local_sem.at[6]),
        pltpu.make_async_copy(loss_scale_hbm, loss_scale, local_sem.at[7]),
    ]
    for copy in loads[:2]:
        copy.start()

    barrier = pltpu.get_barrier_semaphore()
    partners = [at(core=1 - c)]
    partners += [at(dy=1), at(dy=-1), at(dz=1), at(dz=-1)]
    partners += [at(dy=-k * sgn) for k in (-2, 2)]
    partners += [at(dz=-2 * sgn)] + [at(dx=r) for r in (1, 2, 3)]
    for partner in partners:
        pl.semaphore_signal(barrier, inc=1, device_id=partner, device_id_type=MESH)

    for copy in loads[2:]:
        copy.start()

    tags = Tags()
    left = {}

    def send(key, src, dst, device, lane=0):
        index = tags(key)
        assert index < MESSAGES
        pltpu.make_async_remote_copy(
            src, dst, send_sem.at[lane], recv_sem.at[index], device_id=device, device_id_type=MESH
        ).start()
        left[lane] = left.get(lane, 0) + math.prod(src.shape) * src.dtype.itemsize // 4096

    def arrive(key, dst):
        sem = recv_sem.at[tags(key)]
        pltpu.make_async_remote_copy(dst, dst, send_sem.at[0], sem, device_id=sibling, device_id_type=MESH).wait_recv()

    def gone(lane, units):
        view = room.at[pl.ds(0, units)]
        sem = send_sem.at[lane]
        pltpu.make_async_remote_copy(view, view, sem, recv_sem.at[0], device_id=sibling, device_id_type=MESH).wait_send()

    sibling = at(core=1 - c)

    loads[0].wait()
    loads[1].wait()
    t_wide = ts[...].astype(f32)
    t_rad = jnp.sqrt(jnp.sum(t_wide * t_wide, axis=1, keepdims=True) + epsilon)
    t_unit = t_wide / t_rad
    sb[0, 0] = t_unit.astype(bf16)
    q_wide = tt[...].astype(f32)
    tb[0, 0] = (q_wide / jnp.sqrt(jnp.sum(q_wide * q_wide, axis=1, keepdims=True) + epsilon)).astype(bf16)

    pl.semaphore_wait(barrier, len(partners))

    z_to = {1: at(dz=sgn), -1: at(dz=-sgn)}

    def s_part(pos, part):
        return sb.at[pos, pl.ds(0, 3)] if part == 0 else sb.at[pos, pl.ds(3, 1)]

    def t_group(b, group):
        start, count = GROUPS[group]
        return tb.at[b, pl.ds(start, count)]

    def gather_message(key):
        kind = key[0]
        if kind == "ty":
            pos = key[1]
            before, far = T_TREE[pos]
            return [("ty", before)], tb.at[0, before], tb.at[0, pos], at(dy=FLOW[pos][1] * far * sgn)
        if kind == "sy":
            pos, part = key[1:]
            before, far = S_TREES[part][pos]
            parents = [("sy", before, part)] if before else [[("sz", 1)], [("sz", 3)]][part]
            return parents, s_part(before, part), s_part(pos, part), at(dy=FLOW[pos][1] * far * sgn)
        if kind == "sz":
            b = key[1]
            return [], sb.at[0, 0], sb.at[0, b], at(dz=ZFLOW[b] * sgn)
        b, group = key[1:]
        start, count = GROUPS[group]
        if b == 3 and group not in LONG:
            return [("tz", 1, group)], t_group(1, group), t_group(3, group), z_to[1]
        return [("ty", pos) for pos in range(start, start + count)], t_group(0, group), t_group(b, group), at(dz=ZFLOW[b] * sgn)

    waited = {("ty", 0)}

    def need(key):
        if key in waited:
            return
        waited.add(key)
        kind = key[0]
        if kind == "ty":
            arrive(key, tb.at[0, key[1]])
        elif kind == "sy":
            arrive(key, s_part(key[1], key[2]))
        elif kind == "sz":
            arrive(key, sb.at[0, pl.ds(1, 2)] if key[1] == 1 else s_part(0, 1))
        elif key[1] == 1:
            arrive(key, t_group(1, key[2]))
        else:
            start, count = GROUPS[key[2]]
            arrive(key, tb.at[pl.ds(2, 2), pl.ds(start, count)])

    def pass_on(key):
        parents, src, dst, device = gather_message(key)
        for parent in parents:
            need(parent)
        if key[0] == "tz" and key[1] == 3:
            key = ("tz", 2, key[2])
        if key == ("sz", 2):
            key = ("sz", 1)
        send(key, src, dst, device)

    def prepare(k):
        projected = jnp.dot(xall[k], w[...], preferred_element_type=f32)
        radius = jnp.sqrt(jnp.sum(projected * projected, axis=1, keepdims=True) + epsilon)
        u = projected / radius
        here = pl.ds(128 * k, 128)
        for j in range(6):
            unit[j, here] = u[:, 128 * j : 128 * (j + 1)]
        rad[here] = 1.0 / radius
        low[k] = u.astype(bf16)
        v = xtall[k].astype(f32)
        teach[k] = (v / jnp.sqrt(jnp.sum(v * v, axis=1, keepdims=True) + epsilon)).astype(bf16)

    def turn():
        for k in range(2):
            flat = xall[k].astype(f32).T
            for yy in range(8):
                rows = [flat[zl * 192 + yy * 24 : zl * 192 + yy * 24 + 24] for zl in range(4)]
                xtp[yy, :, 128 * k : 128 * (k + 1)] = jnp.concatenate(rows, axis=0).astype(bf16)

    def tile(group):
        start, count = GROUPS[group]
        for pos in range(start, start + count):
            need(("ty", pos))
            for part in range(2):
                if pos:
                    need(("sy", pos, part))
        for key in [("sz", 1), ("sz", 3), ("tz", 1, group), ("tz", 2, group)]:
            need(key)
        n = count * 64
        rows = sb[start : start + count].reshape(n, 768)
        teach_rows = jnp.concatenate([tb[:, p].reshape(64, 1152) for p in range(start, start + count)], axis=0)
        low_all = low[...].reshape(256, 768)
        student = scales[0] * contract_last(rows, low_all) + biases[0]
        teacher = scales[1] * contract_last(teach_rows, teach[...].reshape(256, 1152)) + biases[1]
        target = 1.0 / (1.0 + jnp.exp(-teacher))
        small = jnp.exp(-jnp.abs(student))
        inverse = 1.0 / (1.0 + small)
        sig = jnp.where(student >= 0.0, inverse, small * inverse)
        loss = jnp.maximum(student, 0.0) + jnp.log1p(small) - target * student
        errors = (sig - target).astype(bf16)
        part = jnp.sum(loss, axis=0, keepdims=True)
        gradient = contract_first(errors, rows)
        if group == 0:
            lpart[...] = part
        else:
            lpart[...] += part
        for j in range(6):
            columns = gradient[:, 128 * j : 128 * (j + 1)]
            grad[j] = columns if group == 0 else grad[j] + columns
        kept[start : start + count] = errors.reshape(count, 64, 256)

    def terms():
        term = jnp.dot(kept[...].reshape(512, 256), low[...].reshape(256, 768), preferred_element_type=f32)
        term = term.reshape(8, 4, 16, 768)
        town[...] = term[:, 0]
        for b in (1, 2, 3):
            zs[b - 1] = term[:, b].astype(bf16)

    def back_z():
        for b in (3, 1, 2):
            send("gz", zs.at[b - 1], zr.at[b - 1], at(dz=-ZFLOW[b] * sgn))

    def sum_z():
        arrive("gz", zr)
        total = town[...]
        for b in range(3):
            total = total + zr[b].astype(f32)
        town[...] = total
        ysend[...] = total.astype(bf16)

    def back_y(pos):
        steps, sign = FLOW[pos]
        send("gy", ysend.at[pos], yr.at[pos - 1], at(dy=-steps * sign * sgn))

    for action in ORDER:
        kind = action[0]
        if kind == "images":
            loads[2].wait()
            loads[3].wait()
            send("imgs", xall.at[c], xall.at[c], sibling)
            send("imgt", xtall.at[c], xtall.at[c], sibling)
            for copy in loads[4:]:
                copy.wait()
        elif kind == "prepare":
            if action[1] == 1:
                arrive("imgs", xall.at[1 - c])
                arrive("imgt", xtall.at[1 - c])
            prepare(c if action[1] == 0 else 1 - c)
        elif kind == "turn":
            turn()
        elif kind == "tile":
            tile(action[1])
        else:
            pass_on(action)
    tile(4)

    factor = loss_scale[0] * scales[0] / 8192.0
    radial = grad[0] * unit[0]
    for j in range(1, 6):
        radial = radial + grad[j] * unit[j]
    radial = jnp.sum(radial, axis=1, keepdims=True)
    over = rad[...] * factor

    def step(j):
        return (grad[j] - unit[j] * radial) * over

    for j in range(3):
        csend[j] = step(3 * (1 - c) + j).astype(bf16)
        send(("cs", j), csend.at[j], crecv.at[j], sibling)
    for j in range(3):
        csum[j] = step(3 * c + j)
    for k in range(2):
        lc[k] = jnp.broadcast_to(lpart[:, 128 * k : 128 * (k + 1)], (8, 128))
    send("cl", lc.at[1 - c], lc.at[2], sibling)

    for j in range(3):
        arrive(("cs", j), crecv.at[j])
        total = csum[j] + crecv[j].astype(f32)

        @pl.when(x == j)
        def _():
            csum[j] = total

        @pl.when(x != j)
        def _():
            sx[j] = total.astype(bf16)
            send("xs", sx.at[j], xr.at[lax.rem(j - x + 4, 4) - 1], at(dx=j - x), lane=1 + j)

    terms()
    back_z()
    arrive("cl", lc.at[2])
    lx[...] = lc[c] + lc[2]
    for r in (2, 1, 3):
        send("xl", lx, lxr.at[r - 1], at(dx=r))

    @pl.when(x < 3)
    def _():
        arrive("xs", xr)
        s = csum[x] + xr[0].astype(f32) + xr[1].astype(f32) + xr[2].astype(f32)
        high = s.astype(bf16)
        both = jnp.concatenate([high, (s - high.astype(f32)).astype(bf16)], axis=1)
        for half in ((4, 3, 5, 2), (6, 1, 7, 0)):
            turned = jnp.concatenate([xtp[lax.rem(y + r, 8)] for r in half], axis=0)
            product = jnp.dot(turned, both, preferred_element_type=f32)
            h = (product[:, :128] + product[:, 128:]).reshape(4, 96, 128)
            for place, r in enumerate(half):
                if r == 0:
                    hsum[...] = h[place]
                else:
                    hb[r - 1] = h[place].astype(bf16)
                    send("hy", hb.at[r - 1], hr.at[r - 1], at(dy=r), lane=4)

    arrive("xl", lxr)
    lh[0] = lx[...] + lxr[0] + lxr[1] + lxr[2]
    send("hl", lh.at[0], lh.at[1], at(dz=4))
    sum_z()

    @pl.when(x < 3)
    def _():
        arrive("hy", hr)
        total = hsum[...]
        for r in range(1, 8):
            total = total + hr[r - 1].astype(f32)
        zb[...] = total.reshape(4, 24, 128)
        for r in (4, 3, 5, 2, 6, 1, 7):
            send("hz", zb.at[lax.rem(z + r, 4)], zrec.at[r - 1], at(dz=r), lane=4)

    for pos in range(7, 0, -1):
        back_y(pos)
    arrive("hl", lh.at[1])
    loss_out[...] = (lh[0, 0:1] + lh[1, 0:1]) * (1.0 / 8192.0)

    mine = 3 * c + lax.rem(x, 3)

    @pl.when(x < 3)
    def _():
        arrive("hz", zrec)
        total = zb[lax.rem(z, 4)]
        for r in range(1, 8):
            total = total + zrec[r - 1]
        agsend[0] = total[0:16]
        agsend[1] = total[8:24]
        ag[mine] = agsend[c]
        for r in (2, 1, 3):
            for k in (0, 1):
                send("ag", agsend.at[k], ag.at[mine], at(dx=r, core=k), lane=4)
        send("ag", agsend.at[1 - c], ag.at[mine], sibling, lane=4)

    arrive("gy", yr)
    tg = town[0]
    for pos in range(1, 8):
        tg = tg + yr[pos - 1].astype(f32)
    tg = tg * factor
    tw = ts[...].astype(f32)
    tr = jnp.sqrt(jnp.sum(tw * tw, axis=1, keepdims=True) + epsilon)
    tu = tw / tr
    text_out[...] = (tg - tu * jnp.sum(tg * tu, axis=1, keepdims=True)) / tr

    @pl.when(x < 3)
    def _():
        arrive("ag", ag.at[pl.ds(0, 5)])

    @pl.when(x == 3)
    def _():
        arrive("ag", ag)

    for j in range(6):
        head_out[:, 128 * j : 128 * (j + 1)] = jnp.where(c == 0, ag[j, 0:12], ag[j, 4:16])

    gone(0, left[0])
    for j in range(3):

        @pl.when(x != j)
        def _():
            gone(1 + j, left[1 + j])

    @pl.when(x < 3)
    def _():
        gone(4, left[4])


def shards(image_student, head_weight, text_student, image_teacher, text_teacher, logit_scales, logit_biases, loss_scale):
    vm = pltpu.VMEM
    scratch = [
        vm((2, 128, 768), bf16),
        vm((2, 128, 1152), bf16),
        vm((768, 768), bf16),
        vm((16, 768), bf16),
        vm((16, 1152), bf16),
        vm((8, 4, 16, 768), bf16),
        vm((4, 8, 16, 1152), bf16),
        vm((6, 256, 128), f32),
        vm((2, 128, 768), bf16),
        vm((256, 1), f32),
        vm((2, 128, 1152), bf16),
        vm((8, 96, 256), bf16),
        vm((8, 64, 256), bf16),
        vm((8, 16, 768), f32),
        vm((3, 8, 16, 768), bf16),
        vm((3, 8, 16, 768), bf16),
        vm((8, 16, 768), bf16),
        vm((7, 16, 768), bf16),
        vm((6, 256, 128), f32),
        vm((3, 256, 128), bf16),
        vm((3, 256, 128), bf16),
        vm((3, 256, 128), f32),
        vm((3, 256, 128), bf16),
        vm((3, 256, 128), bf16),
        vm((96, 128), f32),
        vm((7, 96, 128), bf16),
        vm((7, 96, 128), bf16),
        vm((4, 24, 128), f32),
        vm((7, 24, 128), f32),
        vm((2, 16, 128), f32),
        vm((6, 16, 128), f32),
        vm((1, 256), f32),
        vm((3, 8, 128), f32),
        vm((8, 128), f32),
        vm((3, 8, 128), f32),
        vm((2, 8, 128), f32),
        vm((ROOM, 8, 128), f32),
        pltpu.SMEM((2,), f32),
        pltpu.SMEM((2,), f32),
        pltpu.SMEM((1,), f32),
        pltpu.SemaphoreType.DMA((8,)),
        pltpu.SemaphoreType.DMA((5,)),
        pltpu.SemaphoreType.DMA((MESSAGES,)),
    ]
    hbm = pl.BlockSpec(memory_space=pltpu.HBM)
    vmem = pl.BlockSpec(memory_space=pltpu.VMEM)
    head, text, loss = pl.pallas_call(
        kernel,
        out_shape=(
            pltpu.VMEM((12, 768), f32),
            pltpu.VMEM((16, 768), f32),
            pltpu.VMEM((1, 128), f32),
        ),
        in_specs=[hbm] * 8,
        out_specs=(vmem, vmem, vmem),
        scratch_shapes=scratch,
        compiler_params=pltpu.CompilerParams(collective_id=0, has_side_effects=True, vmem_limit_bytes=60 * 1024 * 1024),
        name="distill",
    )(image_student, head_weight, text_student, image_teacher, text_teacher, logit_scales, logit_biases, loss_scale)
    return head, text, loss.reshape(128)


def solution(mesh):
    placed = (
        P("blk", None), P(), P(("blk", "txt"), None), P("blk", None), P(("blk", "txt"), None), P(), P(), P(),
    )
    return jax.shard_map(
        shards,
        mesh=mesh,
        in_specs=placed,
        out_specs=(P("blk", None), P(("blk", "txt"), None), P("blk")),
        check_vma=False,
    )
```

```python
import math

import jax
import jax.numpy as jnp
from jax import lax
from jax.experimental import pallas as pl
from jax.experimental.pallas import tpu as pltpu
from jax.sharding import PartitionSpec as P

epsilon = 1e-06
MESH = pl.DeviceIdType.MESH
f32 = jnp.float32
bf16 = jnp.bfloat16

FLOW = {1: (1, 1), 2: (1, -1), 3: (2, 1), 4: (2, -1), 5: (3, 1), 6: (3, -1), 7: (4, 1)}
T_TREE = {1: (0, 1), 2: (0, 1), 3: (0, 2), 4: (0, 2), 5: (1, 2), 6: (4, 1), 7: (5, 1)}
S_TREES = [
    {1: (0, 1), 2: (0, 1), 3: (1, 1), 4: (2, 1), 5: (3, 1), 6: (4, 1), 7: (3, 2)},
    {1: (0, 1), 2: (0, 1), 3: (0, 2), 4: (0, 2), 5: (1, 2), 6: (2, 2), 7: (3, 2)},
]
LONG = (0, 3)
GROUPS = [(0, 1), (1, 2), (3, 2), (5, 2), (7, 1)]
ZFLOW = {1: 1, 2: -1, 3: 2}
ORDER = [
    ("ty", 1), ("sz", 1), ("sz", 2), ("ty", 4), ("ty", 3), ("ty", 2), ("sz", 3), ("tz", 3, 0), ("tz", 1, 0), ("tz", 2, 0),
    ("images",), ("prepare", 0), ("prepare", 1), ("ty", 5), ("turn",), ("sy", 1, 0), ("sy", 2, 0), ("tz", 1, 1),
    ("tz", 2, 1), ("ty", 6), ("tz", 1, 2), ("sy", 3, 1), ("sy", 1, 1), ("sy", 2, 1), ("tz", 2, 2), ("sy", 4, 1), ("tile", 0),
    ("ty", 7), ("sy", 3, 0), ("sy", 4, 0), ("tz", 3, 1), ("tz", 3, 3), ("tz", 1, 3), ("tz", 2, 3), ("sy", 5, 1),
    ("sy", 6, 1), ("tz", 3, 2), ("tz", 1, 4), ("sy", 7, 1), ("tz", 2, 4), ("sy", 7, 0), ("sy", 5, 0), ("sy", 6, 0),
    ("tile", 1), ("tz", 3, 4), ("tile", 2), ("tile", 3),
]


def contract_last(a, b):
    return lax.dot_general(a, b, (((1,), (1,)), ((), ())), preferred_element_type=f32)


def contract_first(a, b):
    return lax.dot_general(a, b, (((0,), (0,)), ((), ())), preferred_element_type=f32)


class Tags:
    def __init__(self):
        self.index = {}

    def __call__(self, key):
        return self.index.setdefault(key, len(self.index))


MESSAGES = 47
ROOM = 2048


def kernel(
    x_hbm, w_hbm, ts_hbm, xt_hbm, tt_hbm, scales_hbm, biases_hbm, loss_scale_hbm,
    head_out, text_out, loss_out,
    xall, xtall, w, ts, tt, sb, tb, unit, low, rad, teach, xtp,
    kept, town, zs, zr, ysend, yr, grad, csend, crecv, csum, sx, xr, hsum, hb, hr, zb, zrec, agsend, ag, lpart, lc, lx, lxr, lh,
    room, scales, biases, loss_scale, local_sem, send_sem, recv_sem,
):
    blk = lax.axis_index("blk")
    txt = lax.axis_index("txt")
    x = lax.rem(txt, 4)
    c = lax.rem(blk, 2)
    y = lax.rem(blk // 2, 8)
    z = (txt // 4) * 4 + blk // 16
    sgn = 2 * c - 1

    def at(dx=0, dy=0, dz=0, core=c):
        xx = lax.rem(x + dx + 8, 4)
        yy = lax.rem(y + dy + 16, 8)
        zz = lax.rem(z + dz + 16, 8)
        return {"blk": (lax.rem(zz, 4) * 8 + yy) * 2 + core, "txt": (zz // 4) * 4 + xx}

    loads = [
        pltpu.make_async_copy(ts_hbm, ts, local_sem.at[0]),
        pltpu.make_async_copy(tt_hbm, tt, local_sem.at[1]),
        pltpu.make_async_copy(x_hbm, xall.at[c], local_sem.at[2]),
        pltpu.make_async_copy(xt_hbm, xtall.at[c], local_sem.at[3]),
        pltpu.make_async_copy(w_hbm, w, local_sem.at[4]),
        pltpu.make_async_copy(scales_hbm, scales, local_sem.at[5]),
        pltpu.make_async_copy(biases_hbm, biases, local_sem.at[6]),
        pltpu.make_async_copy(loss_scale_hbm, loss_scale, local_sem.at[7]),
    ]
    barrier = pltpu.get_barrier_semaphore()
    partners = [at(dx=2), at(dy=2), at(dy=-2), at(dz=-2 * sgn)]
    partners += [at(dx=1), at(dx=3), at(dy=1), at(dy=-1), at(dz=1), at(dz=-1), at(core=1 - c)]
    for partner in partners:
        pl.semaphore_signal(barrier, inc=1, device_id=partner, device_id_type=MESH)

    for copy in loads:
        copy.start()

    tags = Tags()
    left = {}

    def send(key, src, dst, device, lane=0):
        index = tags(key)
        assert index < MESSAGES
        pltpu.make_async_remote_copy(
            src, dst, send_sem.at[lane], recv_sem.at[index], device_id=device, device_id_type=MESH
        ).start()
        left[lane] = left.get(lane, 0) + math.prod(src.shape) * src.dtype.itemsize // 4096

    def arrive(key, dst):
        sem = recv_sem.at[tags(key)]
        pltpu.make_async_remote_copy(dst, dst, send_sem.at[0], sem, device_id=sibling, device_id_type=MESH).wait_recv()

    def gone(lane, units):
        view = room.at[pl.ds(0, units)]
        sem = send_sem.at[lane]
        pltpu.make_async_remote_copy(view, view, sem, recv_sem.at[0], device_id=sibling, device_id_type=MESH).wait_send()

    sibling = at(core=1 - c)

    loads[0].wait()
    loads[1].wait()
    t_wide = ts[...].astype(f32)
    t_rad = jnp.sqrt(jnp.sum(t_wide * t_wide, axis=1, keepdims=True) + epsilon)
    t_unit = t_wide / t_rad
    sb[0, 0] = t_unit.astype(bf16)
    q_wide = tt[...].astype(f32)
    tb[0, 0] = (q_wide / jnp.sqrt(jnp.sum(q_wide * q_wide, axis=1, keepdims=True) + epsilon)).astype(bf16)

    pl.semaphore_wait(barrier, len(partners))

    z_to = {1: at(dz=sgn), -1: at(dz=-sgn)}

    def s_part(pos, part):
        return sb.at[pos, pl.ds(0, 3)] if part == 0 else sb.at[pos, pl.ds(3, 1)]

    def t_group(b, group):
        start, count = GROUPS[group]
        return tb.at[b, pl.ds(start, count)]

    def gather_message(key):
        kind = key[0]
        if kind == "ty":
            pos = key[1]
            before, far = T_TREE[pos]
            return [("ty", before)], tb.at[0, before], tb.at[0, pos], at(dy=FLOW[pos][1] * far * sgn)
        if kind == "sy":
            pos, part = key[1:]
            before, far = S_TREES[part][pos]
            parents = [("sy", before, part)] if before else [[("sz", 1)], [("sz", 3)]][part]
            return parents, s_part(before, part), s_part(pos, part), at(dy=FLOW[pos][1] * far * sgn)
        if kind == "sz":
            b = key[1]
            return [], sb.at[0, 0], sb.at[0, b], at(dz=ZFLOW[b] * sgn)
        b, group = key[1:]
        start, count = GROUPS[group]
        if b == 3 and group not in LONG:
            return [("tz", 1, group)], t_group(1, group), t_group(3, group), z_to[1]
        return [("ty", pos) for pos in range(start, start + count)], t_group(0, group), t_group(b, group), at(dz=ZFLOW[b] * sgn)

    waited = {("ty", 0)}

    def need(key):
        if key in waited:
            return
        waited.add(key)
        kind = key[0]
        if kind == "ty":
            arrive(key, tb.at[0, key[1]])
        elif kind == "sy":
            arrive(key, s_part(key[1], key[2]))
        elif kind == "sz":
            arrive(key, sb.at[0, pl.ds(1, 2)] if key[1] == 1 else s_part(0, 1))
        elif key[1] == 1:
            arrive(key, t_group(1, key[2]))
        else:
            start, count = GROUPS[key[2]]
            arrive(key, tb.at[pl.ds(2, 2), pl.ds(start, count)])

    def pass_on(key):
        parents, src, dst, device = gather_message(key)
        for parent in parents:
            need(parent)
        if key[0] == "tz" and key[1] == 3:
            key = ("tz", 2, key[2])
        if key == ("sz", 2):
            key = ("sz", 1)
        send(key, src, dst, device)

    def prepare(k):
        projected = jnp.dot(xall[k], w[...], preferred_element_type=f32)
        radius = jnp.sqrt(jnp.sum(projected * projected, axis=1, keepdims=True) + epsilon)
        u = projected / radius
        here = pl.ds(128 * k, 128)
        for j in range(6):
            unit[j, here] = u[:, 128 * j : 128 * (j + 1)]
        rad[here] = 1.0 / radius
        low[k] = u.astype(bf16)
        v = xtall[k].astype(f32)
        teach[k] = (v / jnp.sqrt(jnp.sum(v * v, axis=1, keepdims=True) + epsilon)).astype(bf16)

    def turn():
        for k in range(2):
            flat = xall[k].astype(f32).T
            for yy in range(8):
                rows = [flat[zl * 192 + yy * 24 : zl * 192 + yy * 24 + 24] for zl in range(4)]
                xtp[yy, :, 128 * k : 128 * (k + 1)] = jnp.concatenate(rows, axis=0).astype(bf16)

    def tile(group):
        start, count = GROUPS[group]
        for pos in range(start, start + count):
            need(("ty", pos))
            for part in range(2):
                if pos:
                    need(("sy", pos, part))
        for key in [("sz", 1), ("sz", 3), ("tz", 1, group), ("tz", 2, group)]:
            need(key)
        n = count * 64
        rows = sb[start : start + count].reshape(n, 768)
        teach_rows = jnp.concatenate([tb[:, p].reshape(64, 1152) for p in range(start, start + count)], axis=0)
        low_all = low[...].reshape(256, 768)
        student = scales[0] * contract_last(rows, low_all) + biases[0]
        teacher = scales[1] * contract_last(teach_rows, teach[...].reshape(256, 1152)) + biases[1]
        target = 1.0 / (1.0 + jnp.exp(-teacher))
        small = jnp.exp(-jnp.abs(student))
        inverse = 1.0 / (1.0 + small)
        sig = jnp.where(student >= 0.0, inverse, small * inverse)
        loss = jnp.maximum(student, 0.0) + jnp.log1p(small) - target * student
        errors = (sig - target).astype(bf16)
        part = jnp.sum(loss, axis=0, keepdims=True)
        gradient = contract_first(errors, rows)
        if group == 0:
            lpart[...] = part
        else:
            lpart[...] += part
        for j in range(6):
            columns = gradient[:, 128 * j : 128 * (j + 1)]
            grad[j] = columns if group == 0 else grad[j] + columns
        kept[start : start + count] = errors.reshape(count, 64, 256)

    def terms():
        term = jnp.dot(kept[...].reshape(512, 256), low[...].reshape(256, 768), preferred_element_type=f32)
        term = term.reshape(8, 4, 16, 768)
        town[...] = term[:, 0]
        for b in (1, 2, 3):
            zs[b - 1] = term[:, b].astype(bf16)

    def back_z():
        for b in (3, 1, 2):
            send("gz", zs.at[b - 1], zr.at[b - 1], at(dz=-ZFLOW[b] * sgn))

    def sum_z():
        arrive("gz", zr)
        total = town[...]
        for b in range(3):
            total = total + zr[b].astype(f32)
        town[...] = total
        ysend[...] = total.astype(bf16)

    def back_y(pos):
        steps, sign = FLOW[pos]
        send("gy", ysend.at[pos], yr.at[pos - 1], at(dy=-steps * sign * sgn))

    for action in ORDER:
        kind = action[0]
        if kind == "images":
            loads[2].wait()
            loads[3].wait()
            send("imgs", xall.at[c], xall.at[c], sibling)
            send("imgt", xtall.at[c], xtall.at[c], sibling)
            for copy in loads[4:]:
                copy.wait()
        elif kind == "prepare":
            if action[1] == 1:
                arrive("imgs", xall.at[1 - c])
                arrive("imgt", xtall.at[1 - c])
            prepare(c if action[1] == 0 else 1 - c)
        elif kind == "turn":
            turn()
        elif kind == "tile":
            tile(action[1])
        else:
            pass_on(action)
    tile(4)

    factor = loss_scale[0] * scales[0] / 8192.0
    radial = grad[0] * unit[0]
    for j in range(1, 6):
        radial = radial + grad[j] * unit[j]
    radial = jnp.sum(radial, axis=1, keepdims=True)
    over = rad[...] * factor

    def step(j):
        return (grad[j] - unit[j] * radial) * over

    for j in range(3):
        csend[j] = step(3 * (1 - c) + j).astype(bf16)
        send(("cs", j), csend.at[j], crecv.at[j], sibling)
    for j in range(3):
        csum[j] = step(3 * c + j)
    for k in range(2):
        lc[k] = jnp.broadcast_to(lpart[:, 128 * k : 128 * (k + 1)], (8, 128))
    send("cl", lc.at[1 - c], lc.at[2], sibling)

    for j in range(3):
        arrive(("cs", j), crecv.at[j])
        total = csum[j] + crecv[j].astype(f32)

        @pl.when(x == j)
        def _():
            csum[j] = total

        @pl.when(x != j)
        def _():
            sx[j] = total.astype(bf16)
            send("xs", sx.at[j], xr.at[lax.rem(j - x + 4, 4) - 1], at(dx=j - x), lane=1 + j)

    terms()
    back_z()
    arrive("cl", lc.at[2])
    lx[...] = lc[c] + lc[2]
    for r in (2, 1, 3):
        send("xl", lx, lxr.at[r - 1], at(dx=r))

    @pl.when(x < 3)
    def _():
        arrive("xs", xr)
        s = csum[x] + xr[0].astype(f32) + xr[1].astype(f32) + xr[2].astype(f32)
        high = s.astype(bf16)
        both = jnp.concatenate([high, (s - high.astype(f32)).astype(bf16)], axis=1)
        for half in ((4, 3, 5, 2), (6, 1, 7, 0)):
            turned = jnp.concatenate([xtp[lax.rem(y + r, 8)] for r in half], axis=0)
            product = jnp.dot(turned, both, preferred_element_type=f32)
            h = (product[:, :128] + product[:, 128:]).reshape(4, 96, 128)
            for place, r in enumerate(half):
                if r == 0:
                    hsum[...] = h[place]
                else:
                    hb[r - 1] = h[place].astype(bf16)
                    send("hy", hb.at[r - 1], hr.at[r - 1], at(dy=r), lane=4)

    arrive("xl", lxr)
    lh[0] = lx[...] + lxr[0] + lxr[1] + lxr[2]
    send("hl", lh.at[0], lh.at[1], at(dz=4))
    sum_z()

    @pl.when(x < 3)
    def _():
        arrive("hy", hr)
        total = hsum[...]
        for r in range(1, 8):
            total = total + hr[r - 1].astype(f32)
        zb[...] = total.reshape(4, 24, 128)
        for r in (4, 3, 5, 2, 6, 1, 7):
            send("hz", zb.at[lax.rem(z + r, 4)], zrec.at[r - 1], at(dz=r), lane=4)

    for pos in range(7, 0, -1):
        back_y(pos)
    arrive("hl", lh.at[1])
    loss_out[...] = (lh[0, 0:1] + lh[1, 0:1]) * (1.0 / 8192.0)

    mine = 3 * c + lax.rem(x, 3)

    @pl.when(x < 3)
    def _():
        arrive("hz", zrec)
        total = zb[lax.rem(z, 4)]
        for r in range(1, 8):
            total = total + zrec[r - 1]
        agsend[0] = total[0:16]
        agsend[1] = total[8:24]
        ag[mine] = agsend[c]
        for r in (2, 1, 3):
            for k in (0, 1):
                send("ag", agsend.at[k], ag.at[mine], at(dx=r, core=k), lane=4)
        send("ag", agsend.at[1 - c], ag.at[mine], sibling, lane=4)

    arrive("gy", yr)
    tg = town[0]
    for pos in range(1, 8):
        tg = tg + yr[pos - 1].astype(f32)
    tg = tg * factor
    tw = ts[...].astype(f32)
    tr = jnp.sqrt(jnp.sum(tw * tw, axis=1, keepdims=True) + epsilon)
    tu = tw / tr
    text_out[...] = (tg - tu * jnp.sum(tg * tu, axis=1, keepdims=True)) / tr

    @pl.when(x < 3)
    def _():
        arrive("ag", ag.at[pl.ds(0, 5)])

    @pl.when(x == 3)
    def _():
        arrive("ag", ag)

    for j in range(6):
        head_out[:, 128 * j : 128 * (j + 1)] = jnp.where(c == 0, ag[j, 0:12], ag[j, 4:16])

    gone(0, left[0])
    for j in range(3):

        @pl.when(x != j)
        def _():
            gone(1 + j, left[1 + j])

    @pl.when(x < 3)
    def _():
        gone(4, left[4])


def shards(image_student, head_weight, text_student, image_teacher, text_teacher, logit_scales, logit_biases, loss_scale):
    vm = pltpu.VMEM
    scratch = [
        vm((2, 128, 768), bf16),
        vm((2, 128, 1152), bf16),
        vm((768, 768), bf16),
        vm((16, 768), bf16),
        vm((16, 1152), bf16),
        vm((8, 4, 16, 768), bf16),
        vm((4, 8, 16, 1152), bf16),
        vm((6, 256, 128), f32),
        vm((2, 128, 768), bf16),
        vm((256, 1), f32),
        vm((2, 128, 1152), bf16),
        vm((8, 96, 256), bf16),
        vm((8, 64, 256), bf16),
        vm((8, 16, 768), f32),
        vm((3, 8, 16, 768), bf16),
        vm((3, 8, 16, 768), bf16),
        vm((8, 16, 768), bf16),
        vm((7, 16, 768), bf16),
        vm((6, 256, 128), f32),
        vm((3, 256, 128), bf16),
        vm((3, 256, 128), bf16),
        vm((3, 256, 128), f32),
        vm((3, 256, 128), bf16),
        vm((3, 256, 128), bf16),
        vm((96, 128), f32),
        vm((7, 96, 128), bf16),
        vm((7, 96, 128), bf16),
        vm((4, 24, 128), f32),
        vm((7, 24, 128), f32),
        vm((2, 16, 128), f32),
        vm((6, 16, 128), f32),
        vm((1, 256), f32),
        vm((3, 8, 128), f32),
        vm((8, 128), f32),
        vm((3, 8, 128), f32),
        vm((2, 8, 128), f32),
        vm((ROOM, 8, 128), f32),
        pltpu.SMEM((2,), f32),
        pltpu.SMEM((2,), f32),
        pltpu.SMEM((1,), f32),
        pltpu.SemaphoreType.DMA((8,)),
        pltpu.SemaphoreType.DMA((5,)),
        pltpu.SemaphoreType.DMA((MESSAGES,)),
    ]
    hbm = pl.BlockSpec(memory_space=pltpu.HBM)
    vmem = pl.BlockSpec(memory_space=pltpu.VMEM)
    head, text, loss = pl.pallas_call(
        kernel,
        out_shape=(
            pltpu.VMEM((12, 768), f32),
            pltpu.VMEM((16, 768), f32),
            pltpu.VMEM((1, 128), f32),
        ),
        in_specs=[hbm] * 8,
        out_specs=(vmem, vmem, vmem),
        scratch_shapes=scratch,
        compiler_params=pltpu.CompilerParams(collective_id=0, has_side_effects=True, vmem_limit_bytes=60 * 1024 * 1024),
        name="distill",
    )(image_student, head_weight, text_student, image_teacher, text_teacher, logit_scales, logit_biases, loss_scale)
    return head, text, loss.reshape(128)


def solution(mesh):
    placed = (
        P("blk", None), P(), P(("blk", "txt"), None), P("blk", None), P(("blk", "txt"), None), P(), P(), P(),
    )
    return jax.shard_map(
        shards,
        mesh=mesh,
        in_specs=placed,
        out_specs=(P("blk", None), P(("blk", "txt"), None), P("blk")),
        check_vma=False,
    )
```

```python
import math

import jax
import jax.numpy as jnp
from jax import lax
from jax.experimental import pallas as pl
from jax.experimental.pallas import tpu as pltpu
from jax.sharding import PartitionSpec as P

epsilon = 1e-06
MESH = pl.DeviceIdType.MESH
f32 = jnp.float32
bf16 = jnp.bfloat16

FLOW = {1: (1, 1), 2: (1, -1), 3: (2, 1), 4: (2, -1), 5: (3, 1), 6: (3, -1), 7: (4, 1)}
T_TREE = {1: (0, 1), 2: (0, 1), 3: (0, 2), 4: (0, 2), 5: (1, 2), 6: (4, 1), 7: (5, 1)}
S_TREES = [
    {1: (0, 1), 2: (0, 1), 3: (1, 1), 4: (2, 1), 5: (3, 1), 6: (4, 1), 7: (3, 2)},
    {1: (0, 1), 2: (0, 1), 3: (0, 2), 4: (0, 2), 5: (1, 2), 6: (2, 2), 7: (3, 2)},
]
LONG = (0, 3)
GROUPS = [(0, 1), (1, 2), (3, 2), (5, 2), (7, 1)]
ZFLOW = {1: 1, 2: -1, 3: 2}
ORDER = [
    ("ty", 1), ("sz", 1), ("sz", 2), ("ty", 4), ("ty", 3), ("ty", 2), ("sz", 3), ("tz", 3, 0), ("tz", 1, 0), ("tz", 2, 0),
    ("images",), ("prepare", 0), ("prepare", 1), ("ty", 5), ("turn",), ("sy", 1, 0), ("sy", 2, 0), ("tz", 1, 1),
    ("tz", 2, 1), ("ty", 6), ("tz", 1, 2), ("sy", 3, 1), ("sy", 1, 1), ("sy", 2, 1), ("tz", 2, 2), ("sy", 4, 1), ("tile", 0),
    ("ty", 7), ("sy", 3, 0), ("sy", 4, 0), ("tz", 3, 1), ("tz", 3, 3), ("tz", 1, 3), ("tz", 2, 3), ("sy", 5, 1),
    ("sy", 6, 1), ("tz", 3, 2), ("tz", 1, 4), ("sy", 7, 1), ("tz", 2, 4), ("sy", 7, 0), ("sy", 5, 0), ("sy", 6, 0),
    ("tile", 1), ("tz", 3, 4), ("tile", 2), ("tile", 3),
]


def contract_last(a, b):
    return lax.dot_general(a, b, (((1,), (1,)), ((), ())), preferred_element_type=f32)


def contract_first(a, b):
    return lax.dot_general(a, b, (((0,), (0,)), ((), ())), preferred_element_type=f32)


class Tags:
    def __init__(self):
        self.index = {}

    def __call__(self, key):
        return self.index.setdefault(key, len(self.index))


MESSAGES = 47
ROOM = 2048


def kernel(
    x_hbm, w_hbm, ts_hbm, xt_hbm, tt_hbm, scales_hbm, biases_hbm, loss_scale_hbm,
    head_out, text_out, loss_out,
    xall, xtall, w, ts, tt, sb, tb, unit, low, rad, teach, xtp,
    kept, town, zs, zr, ysend, yr, grad, csum, sx, xr, hsum, hb, hr, zb, zrec, agsend, ag, lpart, lc, lx, lxr, lh,
    room, scales, biases, loss_scale, local_sem, send_sem, recv_sem,
):
    blk = lax.axis_index("blk")
    txt = lax.axis_index("txt")
    x = lax.rem(txt, 4)
    c = lax.rem(blk, 2)
    y = lax.rem(blk // 2, 8)
    z = (txt // 4) * 4 + blk // 16
    sgn = 2 * c - 1

    def at(dx=0, dy=0, dz=0, core=c):
        xx = lax.rem(x + dx + 8, 4)
        yy = lax.rem(y + dy + 16, 8)
        zz = lax.rem(z + dz + 16, 8)
        return {"blk": (lax.rem(zz, 4) * 8 + yy) * 2 + core, "txt": (zz // 4) * 4 + xx}

    loads = [
        pltpu.make_async_copy(ts_hbm, ts, local_sem.at[0]),
        pltpu.make_async_copy(tt_hbm, tt, local_sem.at[1]),
        pltpu.make_async_copy(x_hbm, xall.at[c], local_sem.at[2]),
        pltpu.make_async_copy(xt_hbm, xtall.at[c], local_sem.at[3]),
        pltpu.make_async_copy(w_hbm, w, local_sem.at[4]),
        pltpu.make_async_copy(scales_hbm, scales, local_sem.at[5]),
        pltpu.make_async_copy(biases_hbm, biases, local_sem.at[6]),
        pltpu.make_async_copy(loss_scale_hbm, loss_scale, local_sem.at[7]),
    ]
    barrier = pltpu.get_barrier_semaphore()
    partners = [at(dx=2), at(dy=2), at(dy=-2), at(dz=-2 * sgn)]
    partners += [at(dx=1), at(dx=3), at(dy=1), at(dy=-1), at(dz=1), at(dz=-1), at(core=1 - c)]
    partners += [at(dx=r, core=1 - c) for r in (2, 1, 3)]
    for partner in partners:
        pl.semaphore_signal(barrier, inc=1, device_id=partner, device_id_type=MESH)

    for copy in loads:
        copy.start()

    tags = Tags()
    left = {}

    def send(key, src, dst, device, lane=0):
        index = tags(key)
        assert index < MESSAGES
        pltpu.make_async_remote_copy(
            src, dst, send_sem.at[lane], recv_sem.at[index], device_id=device, device_id_type=MESH
        ).start()
        left[lane] = left.get(lane, 0) + math.prod(src.shape) * src.dtype.itemsize // 4096

    def arrive(key, dst):
        sem = recv_sem.at[tags(key)]
        pltpu.make_async_remote_copy(dst, dst, send_sem.at[0], sem, device_id=sibling, device_id_type=MESH).wait_recv()

    def gone(lane, units):
        view = room.at[pl.ds(0, units)]
        sem = send_sem.at[lane]
        pltpu.make_async_remote_copy(view, view, sem, recv_sem.at[0], device_id=sibling, device_id_type=MESH).wait_send()

    sibling = at(core=1 - c)

    loads[0].wait()
    loads[1].wait()
    t_wide = ts[...].astype(f32)
    t_rad = jnp.sqrt(jnp.sum(t_wide * t_wide, axis=1, keepdims=True) + epsilon)
    t_unit = t_wide / t_rad
    sb[0, 0] = t_unit.astype(bf16)
    q_wide = tt[...].astype(f32)
    tb[0, 0] = (q_wide / jnp.sqrt(jnp.sum(q_wide * q_wide, axis=1, keepdims=True) + epsilon)).astype(bf16)

    pl.semaphore_wait(barrier, len(partners))

    z_to = {1: at(dz=sgn), -1: at(dz=-sgn)}

    def s_part(pos, part):
        return sb.at[pos, pl.ds(0, 3)] if part == 0 else sb.at[pos, pl.ds(3, 1)]

    def t_group(b, group):
        start, count = GROUPS[group]
        return tb.at[b, pl.ds(start, count)]

    def gather_message(key):
        kind = key[0]
        if kind == "ty":
            pos = key[1]
            before, far = T_TREE[pos]
            return [("ty", before)], tb.at[0, before], tb.at[0, pos], at(dy=FLOW[pos][1] * far * sgn)
        if kind == "sy":
            pos, part = key[1:]
            before, far = S_TREES[part][pos]
            parents = [("sy", before, part)] if before else [[("sz", 1)], [("sz", 3)]][part]
            return parents, s_part(before, part), s_part(pos, part), at(dy=FLOW[pos][1] * far * sgn)
        if kind == "sz":
            b = key[1]
            return [], sb.at[0, 0], sb.at[0, b], at(dz=ZFLOW[b] * sgn)
        b, group = key[1:]
        start, count = GROUPS[group]
        if b == 3 and group not in LONG:
            return [("tz", 1, group)], t_group(1, group), t_group(3, group), z_to[1]
        return [("ty", pos) for pos in range(start, start + count)], t_group(0, group), t_group(b, group), at(dz=ZFLOW[b] * sgn)

    waited = {("ty", 0)}

    def need(key):
        if key in waited:
            return
        waited.add(key)
        kind = key[0]
        if kind == "ty":
            arrive(key, tb.at[0, key[1]])
        elif kind == "sy":
            arrive(key, s_part(key[1], key[2]))
        elif kind == "sz":
            arrive(key, sb.at[0, pl.ds(1, 2)] if key[1] == 1 else s_part(0, 1))
        elif key[1] == 1:
            arrive(key, t_group(1, key[2]))
        else:
            start, count = GROUPS[key[2]]
            arrive(key, tb.at[pl.ds(2, 2), pl.ds(start, count)])

    def pass_on(key):
        parents, src, dst, device = gather_message(key)
        for parent in parents:
            need(parent)
        if key[0] == "tz" and key[1] == 3:
            key = ("tz", 2, key[2])
        if key == ("sz", 2):
            key = ("sz", 1)
        send(key, src, dst, device)

    def prepare(k):
        projected = jnp.dot(xall[k], w[...], preferred_element_type=f32)
        radius = jnp.sqrt(jnp.sum(projected * projected, axis=1, keepdims=True) + epsilon)
        u = projected / radius
        here = pl.ds(128 * k, 128)
        for j in range(6):
            unit[j, here] = u[:, 128 * j : 128 * (j + 1)]
        rad[here] = 1.0 / radius
        low[k] = u.astype(bf16)
        v = xtall[k].astype(f32)
        teach[k] = (v / jnp.sqrt(jnp.sum(v * v, axis=1, keepdims=True) + epsilon)).astype(bf16)

    def turn():
        for k in range(2):
            flat = xall[k].astype(f32).T
            for yy in range(8):
                rows = [flat[zl * 192 + yy * 24 : zl * 192 + yy * 24 + 24] for zl in range(4)]
                xtp[yy, :, 128 * k : 128 * (k + 1)] = jnp.concatenate(rows, axis=0).astype(bf16)

    def tile(group):
        start, count = GROUPS[group]
        for pos in range(start, start + count):
            need(("ty", pos))
            for part in range(2):
                if pos:
                    need(("sy", pos, part))
        for key in [("sz", 1), ("sz", 3), ("tz", 1, group), ("tz", 2, group)]:
            need(key)
        n = count * 64
        rows = sb[start : start + count].reshape(n, 768)
        teach_rows = jnp.concatenate([tb[:, p].reshape(64, 1152) for p in range(start, start + count)], axis=0)
        low_all = low[...].reshape(256, 768)
        student = scales[0] * contract_last(rows, low_all) + biases[0]
        teacher = scales[1] * contract_last(teach_rows, teach[...].reshape(256, 1152)) + biases[1]
        target = 1.0 / (1.0 + jnp.exp(-teacher))
        small = jnp.exp(-jnp.abs(student))
        inverse = 1.0 / (1.0 + small)
        sig = jnp.where(student >= 0.0, inverse, small * inverse)
        loss = jnp.maximum(student, 0.0) + jnp.log1p(small) - target * student
        errors = (sig - target).astype(bf16)
        part = jnp.sum(loss, axis=0, keepdims=True)
        gradient = contract_first(errors, rows)
        if group == 0:
            lpart[...] = part
        else:
            lpart[...] += part
        for j in range(6):
            columns = gradient[:, 128 * j : 128 * (j + 1)]
            grad[j] = columns if group == 0 else grad[j] + columns
        kept[start : start + count] = errors.reshape(count, 64, 256)

    def terms():
        term = jnp.dot(kept[...].reshape(512, 256), low[...].reshape(256, 768), preferred_element_type=f32)
        term = term.reshape(8, 4, 16, 768)
        town[...] = term[:, 0]
        for b in (1, 2, 3):
            zs[b - 1] = term[:, b].astype(bf16)

    def back_z():
        for b in (3, 1, 2):
            send("gz", zs.at[b - 1], zr.at[b - 1], at(dz=-ZFLOW[b] * sgn))

    def sum_z():
        arrive("gz", zr)
        total = town[...]
        for b in range(3):
            total = total + zr[b].astype(f32)
        town[...] = total
        ysend[...] = total.astype(bf16)

    def back_y(pos):
        steps, sign = FLOW[pos]
        send("gy", ysend.at[pos], yr.at[pos - 1], at(dy=-steps * sign * sgn))

    for action in ORDER:
        kind = action[0]
        if kind == "images":
            loads[2].wait()
            loads[3].wait()
            send("imgs", xall.at[c], xall.at[c], sibling)
            send("imgt", xtall.at[c], xtall.at[c], sibling)
            for copy in loads[4:]:
                copy.wait()
        elif kind == "prepare":
            if action[1] == 1:
                arrive("imgs", xall.at[1 - c])
                arrive("imgt", xtall.at[1 - c])
            prepare(c if action[1] == 0 else 1 - c)
        elif kind == "turn":
            turn()
        elif kind == "tile":
            tile(action[1])
        else:
            pass_on(action)
    tile(4)

    factor = loss_scale[0] * scales[0] / 8192.0
    radial = grad[0] * unit[0]
    for j in range(1, 6):
        radial = radial + grad[j] * unit[j]
    radial = jnp.sum(radial, axis=1, keepdims=True)
    over = rad[...] * factor

    def step(j):
        return (grad[j] - unit[j] * radial) * over

    for other in (1, 0):
        for j in (0, 1, 2):
            core = 1 - c if other else c
            columns = step(3 * core + j)
            slot = lax.rem(j - x + 4, 4) * 2 + other - 1
            if other:
                sx[j, 1] = columns.astype(bf16)
                send("xs", sx.at[j, 1], xr.at[slot], at(dx=j - x, core=core))
            else:

                @pl.when(x == j)
                def _():
                    csum[...] = columns

                @pl.when(x != j)
                def _():
                    sx[j, 0] = columns.astype(bf16)
                    send("xs", sx.at[j, 0], xr.at[slot], at(dx=j - x), lane=1 + j)

    for k in range(2):
        lc[k] = jnp.broadcast_to(lpart[:, 128 * k : 128 * (k + 1)], (8, 128))
    send("cl", lc.at[1 - c], lc.at[2], sibling)

    terms()
    back_z()
    arrive("cl", lc.at[2])
    lx[...] = lc[c] + lc[2]
    for r in (2, 1, 3):
        send("xl", lx, lxr.at[r - 1], at(dx=r))

    @pl.when(x < 3)
    def _():
        arrive("xs", xr)
        s = csum[...]
        for i in range(7):
            s = s + xr[i].astype(f32)
        high = s.astype(bf16)
        both = jnp.concatenate([high, (s - high.astype(f32)).astype(bf16)], axis=1)
        for half in ((4, 3, 5, 2), (6, 1, 7, 0)):
            turned = jnp.concatenate([xtp[lax.rem(y + r, 8)] for r in half], axis=0)
            product = jnp.dot(turned, both, preferred_element_type=f32)
            h = (product[:, :128] + product[:, 128:]).reshape(4, 96, 128)
            for place, r in enumerate(half):
                if r == 0:
                    hsum[...] = h[place]
                else:
                    hb[r - 1] = h[place].astype(bf16)
                    send("hy", hb.at[r - 1], hr.at[r - 1], at(dy=r), lane=4)

    arrive("xl", lxr)
    lh[0] = lx[...] + lxr[0] + lxr[1] + lxr[2]
    send("hl", lh.at[0], lh.at[1], at(dz=4))
    sum_z()

    @pl.when(x < 3)
    def _():
        arrive("hy", hr)
        total = hsum[...]
        for r in range(1, 8):
            total = total + hr[r - 1].astype(f32)
        zb[...] = total.reshape(4, 24, 128)
        for r in (4, 3, 5, 2, 6, 1, 7):
            send("hz", zb.at[lax.rem(z + r, 4)], zrec.at[r - 1], at(dz=r), lane=4)

    for pos in range(7, 0, -1):
        back_y(pos)
    arrive("hl", lh.at[1])
    loss_out[...] = (lh[0, 0:1] + lh[1, 0:1]) * (1.0 / 8192.0)

    mine = 3 * c + lax.rem(x, 3)

    @pl.when(x < 3)
    def _():
        arrive("hz", zrec)
        total = zb[lax.rem(z, 4)]
        for r in range(1, 8):
            total = total + zrec[r - 1]
        agsend[0] = total[0:16]
        agsend[1] = total[8:24]
        ag[mine] = agsend[c]
        for r in (2, 1, 3):
            for k in (0, 1):
                send("ag", agsend.at[k], ag.at[mine], at(dx=r, core=k), lane=4)
        send("ag", agsend.at[1 - c], ag.at[mine], sibling, lane=4)

    arrive("gy", yr)
    tg = town[0]
    for pos in range(1, 8):
        tg = tg + yr[pos - 1].astype(f32)
    tg = tg * factor
    tw = ts[...].astype(f32)
    tr = jnp.sqrt(jnp.sum(tw * tw, axis=1, keepdims=True) + epsilon)
    tu = tw / tr
    text_out[...] = (tg - tu * jnp.sum(tg * tu, axis=1, keepdims=True)) / tr

    @pl.when(x < 3)
    def _():
        arrive("ag", ag.at[pl.ds(0, 5)])

    @pl.when(x == 3)
    def _():
        arrive("ag", ag)

    for j in range(6):
        head_out[:, 128 * j : 128 * (j + 1)] = jnp.where(c == 0, ag[j, 0:12], ag[j, 4:16])

    gone(0, left[0])
    for j in range(3):

        @pl.when(x != j)
        def _():
            gone(1 + j, left[1 + j])

    @pl.when(x < 3)
    def _():
        gone(4, left[4])


def shards(image_student, head_weight, text_student, image_teacher, text_teacher, logit_scales, logit_biases, loss_scale):
    vm = pltpu.VMEM
    scratch = [
        vm((2, 128, 768), bf16),
        vm((2, 128, 1152), bf16),
        vm((768, 768), bf16),
        vm((16, 768), bf16),
        vm((16, 1152), bf16),
        vm((8, 4, 16, 768), bf16),
        vm((4, 8, 16, 1152), bf16),
        vm((6, 256, 128), f32),
        vm((2, 128, 768), bf16),
        vm((256, 1), f32),
        vm((2, 128, 1152), bf16),
        vm((8, 96, 256), bf16),
        vm((8, 64, 256), bf16),
        vm((8, 16, 768), f32),
        vm((3, 8, 16, 768), bf16),
        vm((3, 8, 16, 768), bf16),
        vm((8, 16, 768), bf16),
        vm((7, 16, 768), bf16),
        vm((6, 256, 128), f32),
        vm((256, 128), f32),
        vm((3, 2, 256, 128), bf16),
        vm((7, 256, 128), bf16),
        vm((96, 128), f32),
        vm((7, 96, 128), bf16),
        vm((7, 96, 128), bf16),
        vm((4, 24, 128), f32),
        vm((7, 24, 128), f32),
        vm((2, 16, 128), f32),
        vm((6, 16, 128), f32),
        vm((1, 256), f32),
        vm((3, 8, 128), f32),
        vm((8, 128), f32),
        vm((3, 8, 128), f32),
        vm((2, 8, 128), f32),
        vm((ROOM, 8, 128), f32),
        pltpu.SMEM((2,), f32),
        pltpu.SMEM((2,), f32),
        pltpu.SMEM((1,), f32),
        pltpu.SemaphoreType.DMA((8,)),
        pltpu.SemaphoreType.DMA((5,)),
        pltpu.SemaphoreType.DMA((MESSAGES,)),
    ]
    hbm = pl.BlockSpec(memory_space=pltpu.HBM)
    vmem = pl.BlockSpec(memory_space=pltpu.VMEM)
    head, text, loss = pl.pallas_call(
        kernel,
        out_shape=(
            pltpu.VMEM((12, 768), f32),
            pltpu.VMEM((16, 768), f32),
            pltpu.VMEM((1, 128), f32),
        ),
        in_specs=[hbm] * 8,
        out_specs=(vmem, vmem, vmem),
        scratch_shapes=scratch,
        compiler_params=pltpu.CompilerParams(collective_id=0, has_side_effects=True, vmem_limit_bytes=60 * 1024 * 1024),
        name="distill",
    )(image_student, head_weight, text_student, image_teacher, text_teacher, logit_scales, logit_biases, loss_scale)
    return head, text, loss.reshape(128)


def solution(mesh):
    placed = (
        P("blk", None), P(), P(("blk", "txt"), None), P("blk", None), P(("blk", "txt"), None), P(), P(), P(),
    )
    return jax.shard_map(
        shards,
        mesh=mesh,
        in_specs=placed,
        out_specs=(P("blk", None), P(("blk", "txt"), None), P("blk")),
        check_vma=False,
    )
```
